32 devices in a mesh: tm: 8 (over y, x, core), freq: 4 (over z).
Axes of the slice: x: 2, y: 2, z: 4, core: 2. Of those that a mesh axis runs over, the one named last changes fastest.
Arguments:
- spectrum: bfloat16 [1024, 6144], P('freq', 'tm'), may hold values from 0.0099487305 to 10
- decay_rate: float32 [1024], P('freq'), may hold values from 1e-07 to 0.03
- init_state: float32 [1024], P('freq'), may hold values from 0.3 to 3
- clip_ids: int32 [6144], P('tm'), may hold values from 0 to 5, never falling along the last dimension, each value on 1 to 2048 neighbouring positions
- encoder: bfloat16 [256, 1024], P(None, 'freq'), may hold values from -0.1875 to 0.1875
- gauss_noise: float32 [256, 6144], P(None, 'tm'), may hold values from -3 to 3
- uniform_noise: float32 [2, 256, 6144], P(None, None, 'tm'), may hold values from 0.02 to 1
- boost_count: int32 [256], replicated, may hold values from 1 to 2
- templates: bfloat16 [1024, 4096], P('freq'), may hold values from 0.0099487305 to 1
Outputs:
- frame_loss: float32 [6144], P('tm')
- template_grad: float32 [4096, 1024], P('tm', 'freq')
The draws below stay inside these ranges and needn't reach their ends.
Inputs may be any that keep to these rules, and one draw needn't show every extreme that they name: `clip_ids`: clip numbers never fall along the frames; each clip holds 1 to 2048 frames, one exactly that many.
All inputs are finite; a program needn't handle non-finite values.
Results may differ from the reference program's by a relative error of at most 0.00033.
Values may be sent and summed in bfloat16 or wider, within the bound.
No kernel may reach another device: no remote copies, remote signals or barrier semaphores. Data moves between devices by JAX's collectives and lax.ppermute only.
A program may use at most 64 MiB of HBM per device.

```python
import math
import jax
import jax.numpy as jnp
import numpy as np
from jax import lax

F = 1024
K = 256
L = 16
CLIPS = 6
TIME = 6144


def with_ends(entries, own_key, low, top_value):
    spot = [jax.random.randint(jax.random.fold_in(own_key, axis), (), 0, length) for axis, length in enumerate(entries.shape)]
    widest = entries.shape.index(max(entries.shape))
    beside = spot[:widest] + [(spot[widest] + 1) % entries.shape[widest]] + spot[widest + 1:]
    return entries.at[tuple(spot)].set(low).at[tuple(beside)].set(top_value)


def block_levels(key, extent, pieces, low, top_value):
    level, own = 1.0, jax.random.fold_in(key, 6)
    for dim, blocks in pieces:
        steps = jnp.exp(jax.random.uniform(jax.random.fold_in(own, dim), (blocks,), jnp.float32, low / len(pieces), top_value / len(pieces)))
        level = level * jnp.repeat(steps, extent[dim] // blocks).reshape([-1 if axis == dim else 1 for axis in range(len(extent))])
    return level


def profile(count, total, most, skew):
    weights = [(1 << 20) // math.isqrt(grade ** skew) + 1 for grade in range(2, count + 1)]
    surplus, holding = total - most - (count - 1), [1] * (count - 1)
    while surplus > 0:
        free = [i for i in range(count - 1) if holding[i] < most]
        mass, remaining = sum([weights[i] for i in free]), surplus
        for i in free:
            extra = min(most - holding[i], max(1, remaining * weights[i] // mass), surplus)
            holding[i] = holding[i] + extra
            surplus = surplus - extra
    return np.array([most] + holding)


def uneven(key, count, total, limit, slope):
    if count == 2:
        one = jax.random.randint(key, (), max(1, total - limit), min(limit, total - 1) + 1)
        return jnp.stack([one, total - one])
    sizes = jnp.asarray(profile(count, total, limit, slope), jnp.int32)
    couples = (count - 1) // 2
    donor, receiver = sizes[1:1 + 2 * couples:2], sizes[2:2 + 2 * couples:2]
    room = jnp.minimum(donor - 1, limit - receiver)
    shifted = jax.random.randint(jax.random.fold_in(key, 1), (couples,), 0, 1 << 20) % (room + 1)
    sizes = sizes.at[1:1 + 2 * couples:2].set(donor - shifted).at[2:2 + 2 * couples:2].set(receiver + shifted)
    return sizes[jax.random.permutation(jax.random.fold_in(key, 2), count)]


def normal_values(key, shape, scale, reach, shards=(), held_as=jnp.bfloat16):
    values = scale * jax.random.normal(key, shape, jnp.float32)
    if shards:
        values = values * block_levels(key, shape, shards, -0.22, 0.18)
    return jnp.clip(values, -reach, reach).astype(held_as)


def setup_inputs(seed: int = 0) -> dict:
    arg_keys = jax.random.split(jax.random.key(seed), 10)
    spectrum = jnp.clip(jnp.exp(math.log(10.0) - 6.912895 * jax.random.uniform(arg_keys[0], (F, TIME), jnp.float32) ** block_levels(arg_keys[0], (F, TIME), ((0, 4), (1, 8)), -0.2, 0.2)), 0.0099487305, 10.0).astype(jnp.bfloat16)
    decay_rate = jnp.clip(jnp.exp(math.log(0.03) - 12.611538 * jax.random.uniform(arg_keys[1], (F,), jnp.float32) ** block_levels(arg_keys[1], (F,), ((0, 4),), -0.2, 0.2)), 1.0000000116860974e-07, 0.03)
    init_state = jnp.clip(jnp.exp(math.log(3.0) - 2.3025851 * jax.random.uniform(arg_keys[2], (F,), jnp.float32) ** block_levels(arg_keys[2], (F,), ((0, 4),), -0.2, 0.2)), 0.3, 3.0)
    clip_ids = jnp.searchsorted(jnp.cumsum(uneven(arg_keys[3], CLIPS, TIME, TIME // 3, 0)), jnp.arange(TIME), side="right").astype(jnp.int32)
    encoder = normal_values(arg_keys[4], (K, F), F ** -0.5, 0.1875, ((1, 4),))
    gauss_noise = normal_values(arg_keys[5], (K, TIME), 1.0, 3.0, ((1, 8),), jnp.float32)
    uniform_noise = jnp.clip(0.02 + 0.98 * jax.random.uniform(arg_keys[6], (2, K, TIME), jnp.float32) ** block_levels(arg_keys[6], (2, K, TIME), ((2, 8),), -0.2, 0.2), 0.02, 1.0)
    boost_count = with_ends(jax.random.randint(arg_keys[7], (K,), 1, 3), jax.random.fold_in(arg_keys[7], 1), 1, 2).astype(jnp.int32)
    templates = jnp.clip(jnp.exp(math.log(1.0) - 4.61031033 * jax.random.uniform(arg_keys[8], (F, K * L), jnp.float32) ** block_levels(arg_keys[8], (F, K * L), ((0, 4),), -0.2, 0.2)), 0.0099487305, 1.0).astype(jnp.bfloat16)
    return {"spectrum": spectrum, "decay_rate": decay_rate, "init_state": init_state, "clip_ids": clip_ids, "encoder": encoder, "gauss_noise": gauss_noise, "uniform_noise": uniform_noise, "boost_count": boost_count, "templates": templates}


def compose(former, latter):
    return (former[0] * latter[0], latter[0] * former[1] + latter[1])

def topic_mixture(logits, gaussian, uniforms, boost_count):
    concentration = jax.nn.softplus(logits) + 0.5
    boosted = boost_count[:, None]
    shape_total = concentration + boosted.astype(jnp.float32)
    offset = shape_total - 1.0 / 3.0
    spread = lax.rsqrt(9.0 * offset)
    linear = 1.0 + spread * gaussian
    gamma_draw = offset * linear * linear * linear * jnp.exp(jnp.log(uniforms[0]) / concentration)
    gamma_draw = gamma_draw * jnp.where(boosted >= 2, jnp.exp(jnp.log(uniforms[1]) / (concentration + 1.0)), 1.0)
    return (gamma_draw / lax.optimization_barrier(jnp.sum(gamma_draw, axis=0, keepdims=True))).astype(jnp.bfloat16)

def reference(spectrum, decay_rate, init_state, clip_ids, encoder, gauss_noise, uniform_noise, boost_count, templates):
    spectral = spectrum.astype(jnp.float32)
    changed = clip_ids[1:] != clip_ids[:-1]
    factor_row = jnp.concatenate([jnp.ones((1,), jnp.float32), jnp.where(changed, 0.8, 1.0).astype(jnp.float32)])
    rates = (1.0 - decay_rate)[:, None] * factor_row[None, :]
    inputs = decay_rate[:, None] * spectral
    running, summed = lax.associative_scan(compose, (rates, inputs), axis=1)
    smooth = running * init_state[:, None] + summed
    normed = (spectral * lax.rsqrt(smooth + 0.1)).astype(jnp.bfloat16)
    logits = jnp.dot(encoder, normed, preferred_element_type=jnp.float32)
    proportions = topic_mixture(logits, gauss_noise, uniform_noise, boost_count)
    block_len = math.gcd(TIME, 1024)
    blocks = TIME // block_len
    scale_factor = F * K / TIME
    theta_pad = jnp.concatenate([jnp.zeros((K, L - 1), jnp.bfloat16), proportions], axis=1)
    clip_pad = jnp.concatenate([jnp.full((L - 1,), -1, jnp.int32), clip_ids.astype(jnp.int32)])

    def one_block(total, index):
        start = (index * block_len).astype(jnp.int32)
        extended = lax.dynamic_slice_in_dim(theta_pad, start, block_len + L - 1, 1)
        clip_ext = lax.dynamic_slice_in_dim(clip_pad, start, block_len + L - 1, 0)
        current = clip_ext[L - 1:]
        lag_rows = []
        mask_rows = []
        for lag in range(L):
            begin = L - 1 - lag
            lag_rows.append(extended[:, begin:begin + block_len])
            mask_rows.append(clip_ext[begin:begin + block_len] == current)
        valid = jnp.stack(mask_rows).astype(jnp.bfloat16)
        stacked = (jnp.stack(lag_rows, axis=1) * valid[None]).reshape(K * L, block_len)
        local_spec = lax.dynamic_slice_in_dim(spectral, start, block_len, 1)
        recon = jnp.dot(templates, stacked, preferred_element_type=jnp.float32)
        recon_sum = lax.optimization_barrier(jnp.sum(recon, axis=0))
        spec_sum = lax.optimization_barrier(jnp.sum(local_spec, axis=0))
        log_sum = lax.optimization_barrier(jnp.sum(local_spec * jnp.log(recon), axis=0))
        frame_loss = jnp.log(recon_sum) - log_sum / spec_sum
        ratio = (scale_factor * (1.0 / recon_sum[None, :] - local_spec / (spec_sum[None, :] * recon))).astype(jnp.bfloat16)
        grad_term = lax.dot_general(stacked, ratio, (((1,), (1,)), ((), ())), preferred_element_type=jnp.float32)
        return (total + grad_term, frame_loss)
    indices = jnp.arange(blocks, dtype=jnp.int32)
    template_grad, losses = lax.scan(one_block, jnp.zeros((K * L, F), jnp.float32), indices)
    return (losses.reshape(TIME), template_grad)
```

```python
import functools

import jax
import jax.numpy as jnp
from jax import lax
from jax.experimental import pallas as pl
from jax.experimental.pallas import tpu as pltpu
from jax.sharding import PartitionSpec as P

F = 1024
K = 256
L = 16
TOP_CLIP = 5
TAIL = 16
LANES = 128
VMEM = pl.BlockSpec(memory_space=pltpu.VMEM)
SMEM = pl.BlockSpec(memory_space=pltpu.SMEM)
f32 = jnp.float32
bf16 = jnp.bfloat16


def call(kernel, name, outs, scratch, *args, scalars=0, limit=48 << 20):
    return pl.pallas_call(
        kernel,
        name=name,
        out_shape=[jax.ShapeDtypeStruct(shape, dtype) for shape, dtype in outs],
        in_specs=[SMEM] * scalars + [VMEM] * (len(args) - scalars),
        out_specs=[VMEM] * len(outs),
        scratch_shapes=[pltpu.VMEM(shape, dtype) for shape, dtype in scratch],
        compiler_params=pltpu.CompilerParams(vmem_limit_bytes=limit),
    )(*args)


def log_keep(decay):
    gap = 1.0 - (1.0 - decay)
    series = gap * (1.0 / 7.0)
    for order in range(6, 0, -1):
        series = gap * (1.0 / order + series)
    return -series


def column(row, lanes=LANES):
    return jnp.transpose(jnp.broadcast_to(row, (lanes, row.shape[1])))


def wide(col, lanes):
    return jnp.concatenate([col] * (lanes // col.shape[1]), axis=1)


def steps_down(size):
    return (size - 1 - lax.broadcasted_iota(jnp.int32, (size, 1), 0)).astype(f32)


def summary_kernel(nf, place, spectrum, decay, clips, encoder, *refs):
    messages, (own, gains, states, tm_message), (frames_first,) = (
        refs[: nf - 1],
        refs[nf - 1 : nf + 3],
        refs[nf + 3 :],
    )
    bins, frames = spectrum.shape
    piece = frames // nf
    here = place[0, 0]
    clip_row = clips[...].astype(f32)
    clip_col = column(clip_row)
    first = clip_row[:, :1]
    gain = jnp.ones_like(clip_col)
    for value in range(1, TOP_CLIP + 1):
        seen = jnp.max(jnp.where(clip_row == value, 1.0, 0.0), axis=1, keepdims=True)
        counts = (seen > 0.0) & (first < value)
        gain = jnp.where(counts & (clip_col >= value), gain * 0.8, gain)
    frames_first[...] = jnp.transpose(spectrum[...].astype(f32))
    rate = decay[...]
    keep = log_keep(rate)
    scaled = frames_first[...] * wide(1.0 / gain, bins) * rate
    weights = jnp.exp(steps_down(piece) * keep)
    state = jnp.zeros((1, bins), f32)
    states[...] = jnp.zeros_like(states)
    for index in range(nf):
        states[index : index + 1, :] = state
        rows = scaled[index * piece : (index + 1) * piece]
        if index < nf - 1:
            state = jnp.exp(piece * keep) * state + jnp.sum(rows * weights, axis=0, keepdims=True)
    body = piece - TAIL
    state = jnp.exp(body * keep) * state + jnp.sum(
        rows[:body] * weights[TAIL:], axis=0, keepdims=True
    )
    states[nf : nf + 1, :] = state
    state = jnp.exp(TAIL * keep) * state + jnp.sum(
        rows[body:] * weights[body:], axis=0, keepdims=True
    )
    tm_message[0:1, :] = state
    for row in range(frames // bins):
        tm_message[row + 1 : row + 2, :] = clip_row[:, row * bins : (row + 1) * bins]
    for step in range(nf):
        target = own if step == 0 else messages[step - 1]
        start = pl.multiple_of((here ^ step) * piece, piece)
        target[0:piece, :] = frames_first[pl.ds(start, piece), :].astype(bf16)
        target[piece : piece + TAIL, :] = frames_first[frames - TAIL :, :].astype(bf16)
        if step:
            target[piece + TAIL :, :] = encoder[...]
    start = pl.multiple_of(here * piece, piece)
    frames_first[:, 0:LANES] = gain
    gains[0:piece, :] = frames_first[pl.ds(start, piece), 0:LANES]
    gains[piece:, :] = gain[frames - TAIL :]


def totals_kernel(templates, spectrum, stats):
    bins, frames = spectrum.shape
    stats[...] = jnp.zeros_like(stats)
    columns = templates.shape[1]
    for row in range(columns // bins):
        part = templates[:, row * bins : (row + 1) * bins].astype(f32)
        stats[row : row + 1, :] = jnp.sum(part, axis=0, keepdims=True)
    for row in range(frames // bins):
        part = spectrum[:, row * bins : (row + 1) * bins].astype(f32)
        at = columns // bins + row
        stats[at : at + 1, :] = jnp.sum(part, axis=0, keepdims=True)


def entry_kernel(nt, nf, place, decay, init, states, stats, *refs):
    pairs, messages, (own, clips_wide), (blocks, gains) = (
        refs[: nt // 2],
        refs[nt // 2 : nt // 2 + nf - 1],
        refs[nt // 2 + nf - 1 : nt // 2 + nf + 1],
        refs[nt // 2 + nf + 1 :],
    )
    bins = decay.shape[1]
    height = blocks.shape[1]
    frames = (height - 1) * bins
    piece = frames // nf
    here, lap = place[0, 0], place[0, 1]
    for index, pair in enumerate(pairs):
        blocks[2 * index] = pair[0:height]
        blocks[2 * index + 1] = pair[height:]
    ids = blocks[:, 1:, :]
    kinds = jnp.zeros((nt, 1, 1), f32)
    for value in range(TOP_CLIP + 1):
        kinds += jnp.max(jnp.where(ids == value, 1.0, 0.0), axis=(1, 2), keepdims=True)
    gain = jnp.ones_like(kinds)
    for value in range(2, TOP_CLIP + 2):
        gain = jnp.where(kinds >= value, gain * 0.8, gain)
    gains[...] = jnp.broadcast_to(gain, gains.shape)
    keep = log_keep(decay[...])
    through = jnp.exp(frames * keep)
    state = init[...]
    for block in range(nt - 1):
        at, after = block ^ lap, (block + 1) ^ lap
        last = blocks[at, height - 1 : height, bins - 1 : bins]
        first = blocks[after, 1:2, 0:1]
        joint = jnp.where(first != last, 0.8, 1.0)
        passed = joint * (gains[at] * (through * state + blocks[at, 0:1, :]))
        state = jnp.where(block < lap, passed, state)
    tail = jnp.exp((frames - TAIL) * keep) * state + states[nf : nf + 1, :]
    for step in range(nf):
        target = own if step == 0 else messages[step - 1]
        other = here ^ step
        power = jnp.exp((other * piece).astype(f32) * keep)
        target[...] = jnp.zeros_like(target)
        target[0:1, :] = power * state + states[pl.ds(other, 1), :]
        target[1:2, :] = tail
        target[2:3, :] = decay[...]
        if step:
            target[8:, :] = stats[...]
    previous = blocks[jnp.maximum(lap - 1, 0) ^ lap, height - 1 : height, bins - LANES : bins]
    clips_wide[:, 0:LANES] = jnp.where(lap > 0, previous, -1.0)
    for row in range(frames // bins):
        low = LANES + row * bins
        clips_wide[:, low : low + bins] = blocks[0, row + 1 : row + 2, :]


def noise_kernel(nf, place, gauss, uniform, boost, normal, first, second, boosts):
    topics, frames = gauss.shape
    piece = frames // nf
    here = place[0, 0]
    width = normal.shape[1]
    counts = wide(column(boost[...].astype(f32)), width)
    boosts[...] = counts
    normal[...] = jnp.zeros_like(normal)
    first[...] = jnp.ones_like(first)
    second[...] = jnp.ones_like(second)
    pairs = ((gauss, normal), (uniform.at[0], first), (uniform.at[1], second))
    for index in range(nf):

        @pl.when(here == index)
        def _():
            for source, target in pairs:
                target[:, 0:piece] = source[:, index * piece : (index + 1) * piece]

    for source, target in pairs:
        target[:, piece : piece + TAIL] = source[:, frames - TAIL :]
    first[...] = jnp.log(first[...])
    second[...] = jnp.where(counts >= 2.0, jnp.log(second[...]), 0.0)


def sampler_kernel(nf, own, encoder, own_state, gains, normal, first, second, boosts, *refs):
    messages, arrivals, (packed, tail), scratch = (
        refs[: nf - 1],
        refs[nf - 1 : 2 * nf - 2],
        refs[2 * nf - 2 : 2 * nf],
        refs[2 * nf :],
    )
    inputs, running, normed = scratch
    rows, bins = own.shape
    piece = rows - TAIL
    segment = piece // 8
    topics, width = normal.shape
    gain = gains[...]
    inverse = 1.0 / gain
    powers = (1 + lax.broadcasted_iota(jnp.int32, (segment, 1), 0)).astype(f32)
    logits = jnp.zeros((topics, width), f32)
    normed[...] = jnp.zeros_like(normed)
    for step in range(nf):
        state = own_state if step == 0 else arrivals[step - 1]
        block = own if step == 0 else messages[step - 1]
        weights = encoder[...] if step == 0 else messages[step - 1][rows:, :]
        for part in range(bins // LANES):
            at = step * (bins // LANES) + part
            lanes = slice(part * LANES, (part + 1) * LANES)
            spectral = block[0:rows, lanes].astype(f32)
            rate = state[2:3, lanes]
            keep = log_keep(rate)
            fade = 1.0 - rate
            inputs[at] = spectral * inverse * rate
            total = jnp.zeros((8, LANES), f32)
            for row in range(segment):
                total = fade * total + inputs[at, pl.ds(row, 8, stride=segment), :]
                running[at, pl.ds(row, 8, stride=segment), :] = total
            carry = state[0:1, lanes]
            through = jnp.exp(segment * keep)
            fading = jnp.exp(powers * keep)
            for index in range(8):
                low = index * segment
                running[at, low : low + segment, :] += fading * carry
                carry = through * carry + total[index : index + 1, :]
            carry = state[1:2, lanes]
            for row in range(piece, rows):
                carry = fade * carry + inputs[at, row : row + 1, :]
                running[at, row : row + 1, :] = carry
            smooth = running[at] * gain
            normed[step, 0:rows, lanes] = (spectral * lax.rsqrt(smooth + 0.1)).astype(bf16)
        logits += lax.dot_general(
            weights, normed[step], (((1,), (1,)), ((), ())), preferred_element_type=f32
        )
    concentration = jnp.maximum(logits, 0.0) + jnp.log1p(jnp.exp(-jnp.abs(logits))) + 0.5
    offset = concentration + boosts[...] - 1.0 / 3.0
    linear = 1.0 + lax.rsqrt(9.0 * offset) * normal[...]
    draw = offset * linear * linear * linear
    draw = draw * jnp.exp(first[...] / concentration + second[...] / (concentration + 1.0))
    proportions = draw / jnp.sum(draw, axis=0, keepdims=True)
    full, rest = piece // LANES, piece % LANES
    for index in range(full):
        tile = proportions[:, index * LANES : (index + 1) * LANES]
        packed[index * topics : (index + 1) * topics, :] = tile.astype(bf16)
    tile = proportions[:, full * LANES : (full + 1) * LANES]
    if rest:
        half = topics // 2
        lane = lax.broadcasted_iota(jnp.int32, (half, LANES), 1)
        joined = jnp.where(lane < rest, tile[:half], pltpu.roll(tile[half:], rest, 1))
        packed[full * topics :, :] = joined.astype(bf16)
    tail[...] = pltpu.roll(tile, LANES - TAIL - rest, 1).astype(bf16)


def gradient_kernel(nt, nf, place, own, rim, clips, templates, spectrum, stats, *refs):
    messages, arrivals, (away, kept, sums), scratch = (
        refs[: nf - 1],
        refs[nf - 1 : 2 * nf - 2],
        refs[2 * nf - 2 : 2 * nf + 1],
        refs[2 * nf + 1 :],
    )
    extended, heads, stacked, valid, recon, ratio = scratch
    bins, frames = spectrum.shape
    here, lap = place[0, 0], place[0, 1]
    piece = frames // nf
    topics = extended.shape[0]
    tile = stacked.shape[1]
    full, rest = piece // LANES, piece % LANES
    extended[:, 0:LANES] = rim[...].astype(f32)
    for step in range(nf):
        source = own if step == 0 else messages[step - 1]
        for index in range(nf):

            @pl.when((here ^ step) == index)
            def _():
                low = LANES + index * piece
                for part in range(full):
                    values = source[part * topics : (part + 1) * topics, :].astype(f32)
                    extended[:, low + part * LANES : low + (part + 1) * LANES] = values
                if rest:
                    values = source[full * topics :, :].astype(f32)
                    low += full * LANES
                    half = topics // 2
                    extended[0:half, low : low + rest] = values[:, 0:rest]
                    extended[half:, low : low + rest] = values[:, rest:]

    total = stats[...]
    for arrival in arrivals:
        total = total + arrival[8:, :]
    columns = templates.shape[1]
    wide_rows = columns // bins
    heads[...] = jnp.zeros_like(heads)
    for row in range(wide_rows):
        value = total[row : row + 1, :]
        for index in range(3):
            rounded = value.astype(bf16)
            heads[index : index + 1, row * bins : (row + 1) * bins] = rounded
            value = value - rounded.astype(f32)
    for row in range(frames // bins):
        at = wide_rows + row
        sums[2:3, row * bins : (row + 1) * bins] = total[at : at + 1, :]
    scale = F * K / (frames * nt)
    group = 32
    for start in range(0, frames, tile):
        span = slice(start, start + LANES + tile)
        ids = jnp.broadcast_to(clips[:, span], (L, LANES + tile))
        shifted = pltpu.roll(ids, 0, 1, stride=1, stride_axis=0)
        valid[...] = jnp.where(shifted == ids, 1.0, 0.0)[:, LANES:]
        for low in range(0, topics, group):

            def one(index, _):
                topic = low + index
                row = extended[pl.ds(topic, 1), span]
                lagged = pltpu.roll(
                    jnp.broadcast_to(row, (L, LANES + tile)), 0, 1, stride=1, stride_axis=0
                )
                at = pl.multiple_of(topic * L, L)
                stacked[pl.ds(at, L), :] = (lagged[:, LANES:] * valid[...]).astype(bf16)
                return 0

            lax.fori_loop(0, group, one, 0, unroll=4)
            part = slice(low * L, (low + group) * L)
            left = jnp.concatenate([templates[:, part], heads[:, part]], axis=0)
            product = jnp.dot(left, stacked[part, :], preferred_element_type=f32)
            if low == 0:
                recon[...] = product
            else:
                recon[...] += product
        here_frames = slice(start, start + tile)
        rebuilt = recon[0:bins, :]
        recon_sum = recon[bins : bins + 1] + recon[bins + 1 : bins + 2] + recon[bins + 2 : bins + 3]
        spectral = spectrum[:, here_frames].astype(f32)
        spec_sum = sums[2:3, here_frames]
        sums[0:1, here_frames] = recon_sum
        sums[1:2, here_frames] = jnp.sum(spectral * jnp.log(rebuilt), axis=0, keepdims=True)
        ratio[...] = (scale * (1.0 / recon_sum - spectral / (spec_sum * rebuilt))).astype(bf16)
        height = away.shape[1]
        for target, side in ((away, 1), (kept, 0)):
            for step in range(nt // 2):
                owner = lap ^ (2 * step + side)
                at = pl.multiple_of(owner * height, height)
                product = lax.dot_general(
                    stacked[pl.ds(at, height), :],
                    ratio[...],
                    (((1,), (1,)), ((), ())),
                    preferred_element_type=f32,
                )
                if start == 0:
                    target[step] = product
                else:
                    target[step] += product


def exchanged(value, axis, step):
    size = lax.axis_size(axis)
    return lax.ppermute(value, axis, [(index, index ^ step) for index in range(size)])


def on_device(
    spectrum,
    decay_rate,
    init_state,
    clip_ids,
    encoder,
    gauss_noise,
    uniform_noise,
    boost_count,
    templates,
):
    nt, nf = lax.axis_size("tm"), lax.axis_size("freq")
    bins, frames = spectrum.shape
    topics = encoder.shape[0]
    columns = templates.shape[1]
    piece = frames // nf
    rows = piece + TAIL
    width = -(-rows // LANES) * LANES
    place = jnp.stack([lax.axis_index("freq"), lax.axis_index("tm")]).astype(jnp.int32)[None]
    decay = decay_rate[None]
    state_rows = -(-(nf + 1) // 8) * 8
    height = 1 + frames // bins

    *messages, own, gains, states, tm_message = call(
        functools.partial(summary_kernel, nf),
        "summary",
        [((rows + topics, bins), bf16)] * (nf - 1)
        + [
            ((rows, bins), bf16),
            ((rows, LANES), f32),
            ((state_rows, bins), f32),
            ((height, bins), f32),
        ],
        [((frames, bins), f32)],
        place,
        spectrum,
        decay,
        clip_ids[None],
        encoder,
        scalars=1,
    )
    messages = [exchanged(messages[step - 1], "freq", step) for step in range(1, nf)]
    pair = jnp.concatenate([tm_message, exchanged(tm_message, "tm", 1)], axis=0)
    pairs = [pair] + [exchanged(pair, "tm", step) for step in range(2, nt, 2)]
    stat_rows = -(-(columns // bins + frames // bins) // 8) * 8
    (stats,) = call(
        totals_kernel, "totals", [((stat_rows, bins), f32)], [], templates, spectrum
    )
    *arrivals, own_state, clips_wide = call(
        functools.partial(entry_kernel, nt, nf),
        "entry",
        [((8 + stat_rows, bins), f32)] * (nf - 1)
        + [((8, bins), f32), ((1, LANES + frames), f32)],
        [((nt, height, bins), f32), ((nt, 1, bins), f32)],
        place,
        decay,
        init_state[None],
        states,
        stats,
        *pairs,
        scalars=1,
    )
    arrivals = [exchanged(arrivals[step - 1], "freq", step) for step in range(1, nf)]
    noises = call(
        functools.partial(noise_kernel, nf),
        "noise",
        [((topics, width), f32)] * 4,
        [],
        place,
        gauss_noise,
        uniform_noise,
        boost_count[None],
        scalars=1,
    )
    packed, tail = call(
        functools.partial(sampler_kernel, nf),
        "sampler",
        [((topics * piece // LANES, LANES), bf16), ((topics, LANES), bf16)],
        [((nf * bins // LANES, rows, LANES), f32)] * 2 + [((nf, width, bins), bf16)],
        own,
        encoder,
        own_state,
        gains,
        *noises,
        *messages,
        *arrivals,
    )
    shares = [exchanged(packed, "freq", step) for step in range(1, nf)]
    rim = lax.ppermute(tail, "tm", [(index, index + 1) for index in range(nt - 1)])
    tile = 768 if frames % 768 == 0 else frames
    height = columns // nt
    away, kept, sums = call(
        functools.partial(gradient_kernel, nt, nf),
        "gradient",
        [((nt // 2, height, bins), f32)] * 2 + [((8, frames), f32)],
        [
            ((topics, LANES + frames), f32),
            ((16, columns), bf16),
            ((columns, tile), bf16),
            ((L, tile), f32),
            ((bins + 16, tile), f32),
            ((bins, tile), bf16),
        ],
        place,
        packed,
        rim,
        clips_wide,
        templates,
        spectrum,
        stats,
        *shares,
        *arrivals,
        scalars=1,
    )
    both = kept + exchanged(away, "tm", 1)
    parts = [exchanged(both[step], "tm", 2 * step) for step in range(1, nt // 2)]
    log_part = sums[1]
    log_sum = log_part + sum(exchanged(log_part, "freq", step) for step in range(1, nf))
    frame_loss = jnp.log(sums[0]) - log_sum / sums[2]
    return (frame_loss, both[0] + sum(parts))


def solution(mesh):
    placed = (
        P("freq", "tm"),
        P("freq"),
        P("freq"),
        P("tm"),
        P(None, "freq"),
        P(None, "tm"),
        P(None, None, "tm"),
        P(),
        P("freq", None),
    )
    return jax.shard_map(
        on_device, mesh=mesh, in_specs=placed, out_specs=(P("tm"), P("tm", "freq")), check_vma=False
    )
```

```python
import functools

import jax
import jax.numpy as jnp
from jax import lax
from jax.experimental import pallas as pl
from jax.experimental.pallas import tpu as pltpu
from jax.sharding import PartitionSpec as P

F = 1024
K = 256
L = 16
TOP_CLIP = 5
TAIL = 16
LANES = 128
VMEM = pl.BlockSpec(memory_space=pltpu.VMEM)
SMEM = pl.BlockSpec(memory_space=pltpu.SMEM)
f32 = jnp.float32
bf16 = jnp.bfloat16


def call(kernel, name, outs, scratch, *args, scalars=0, limit=12 << 20):
    return pl.pallas_call(
        kernel,
        name=name,
        out_shape=[jax.ShapeDtypeStruct(shape, dtype) for shape, dtype in outs],
        in_specs=[SMEM] * scalars + [VMEM] * (len(args) - scalars),
        out_specs=[VMEM] * len(outs),
        scratch_shapes=[pltpu.VMEM(shape, dtype) for shape, dtype in scratch],
        compiler_params=pltpu.CompilerParams(vmem_limit_bytes=limit),
        cost_estimate=pl.CostEstimate(flops=0, bytes_accessed=0, transcendentals=0),
    )(*args)


def log_keep(decay):
    gap = 1.0 - (1.0 - decay)
    series = gap * (1.0 / 7.0)
    for order in range(6, 0, -1):
        series = gap * (1.0 / order + series)
    return -series


def column(row, lanes=LANES):
    return jnp.transpose(jnp.broadcast_to(row, (lanes, row.shape[1])))


def wide(col, lanes):
    return jnp.concatenate([col] * (lanes // col.shape[1]), axis=1)


def steps_down(size):
    return (size - 1 - lax.broadcasted_iota(jnp.int32, (size, 1), 0)).astype(f32)


def summary_kernel(nf, place, *refs):
    sources, messages, (own, gains, states, tm_message, frame_sums), (frames_first, *held, copied) = (
        refs[:3],
        refs[3 : nf + 2],
        refs[nf + 2 : nf + 7],
        refs[nf + 7 :],
    )
    copies = [
        pltpu.make_async_copy(source, target, copied.at[index])
        for index, (source, target) in enumerate(zip(sources, held))
    ]
    for copy in copies:
        copy.start()
    for copy in copies:
        copy.wait()
    spectrum, small, encoder = held
    bins, frames = spectrum.shape
    piece = frames // nf
    here = place[0, 0]
    clip_row = small[:, bins:]
    clip_col = column(clip_row)
    first = clip_row[:, :1]
    gain = jnp.ones_like(clip_col)
    for value in range(1, TOP_CLIP + 1):
        seen = jnp.max(jnp.where(clip_row == value, 1.0, 0.0), axis=1, keepdims=True)
        counts = (seen > 0.0) & (first < value)
        gain = jnp.where(counts & (clip_col >= value), gain * 0.8, gain)
    spectral = spectrum[...].astype(f32)
    frames_first[...] = jnp.transpose(spectral)
    total = jnp.sum(spectral, axis=0, keepdims=True)
    for row in range(frames // bins):
        frame_sums[row : row + 1, :] = total[:, row * bins : (row + 1) * bins]
    rate = small[:, 0:bins]
    keep = log_keep(rate)
    scaled = frames_first[...] * wide(1.0 / gain, bins) * rate
    weights = jnp.exp(steps_down(piece) * keep)
    state = jnp.zeros((1, bins), f32)
    states[...] = jnp.zeros_like(states)
    for index in range(nf):
        states[index : index + 1, :] = state
        rows = scaled[index * piece : (index + 1) * piece]
        if index < nf - 1:
            state = jnp.exp(piece * keep) * state + jnp.sum(rows * weights, axis=0, keepdims=True)
    body = piece - TAIL
    state = jnp.exp(body * keep) * state + jnp.sum(
        rows[:body] * weights[TAIL:], axis=0, keepdims=True
    )
    states[nf : nf + 1, :] = state
    state = jnp.exp(TAIL * keep) * state + jnp.sum(
        rows[body:] * weights[body:], axis=0, keepdims=True
    )
    tm_message[0:1, :] = state
    for row in range(frames // bins):
        tm_message[row + 1 : row + 2, :] = clip_row[:, row * bins : (row + 1) * bins]
    for step in range(nf):
        target = own if step == 0 else messages[step - 1]
        start = pl.multiple_of((here ^ step) * piece, piece)
        target[0:piece, :] = frames_first[pl.ds(start, piece), :].astype(bf16)
        target[piece : piece + TAIL, :] = frames_first[frames - TAIL :, :].astype(bf16)
        if step:
            half = encoder.shape[0] // 2
            low = pl.multiple_of((place[0, 1] & 1) * half, half)
            target[piece + TAIL :, :] = encoder[pl.ds(low, half), :]
    start = pl.multiple_of(here * piece, piece)
    frames_first[:, 0:LANES] = gain
    gains[0:piece, :] = frames_first[pl.ds(start, piece), 0:LANES]
    gains[piece:, :] = gain[frames - TAIL :]


def halves_kernel(rows, *refs):
    messages = refs[len(refs) // 2 : -1]
    half = messages[0].shape[0] - rows
    for index, message in enumerate(messages):
        refs[-1][index * half : (index + 1) * half, :] = message[rows:, :]


def totals_kernel(templates, frame_sums, stats):
    bins, columns = templates.shape
    for row in range(columns // bins):
        part = templates[:, row * bins : (row + 1) * bins].astype(f32)
        stats[row : row + 1, :] = jnp.sum(part, axis=0, keepdims=True)
    stats[columns // bins : columns // bins + frame_sums.shape[0], :] = frame_sums[...]


def entry_kernel(nt, nf, place, decay, init, states, stats, *refs):
    pairs, messages, (own, clips_wide), (blocks, gains) = (
        refs[: nt // 2],
        refs[nt // 2 : nt // 2 + nf - 1],
        refs[nt // 2 + nf - 1 : nt // 2 + nf + 1],
        refs[nt // 2 + nf + 1 :],
    )
    bins = decay.shape[1]
    height = blocks.shape[1]
    frames = (height - 1) * bins
    piece = frames // nf
    here, lap = place[0, 0], place[0, 1]
    for index, pair in enumerate(pairs):
        blocks[2 * index] = pair[0:height]
        blocks[2 * index + 1] = pair[height:]
    ids = blocks[:, 1:, :]
    kinds = jnp.zeros((nt, 1, 1), f32)
    for value in range(TOP_CLIP + 1):
        kinds += jnp.max(jnp.where(ids == value, 1.0, 0.0), axis=(1, 2), keepdims=True)
    gain = jnp.ones_like(kinds)
    for value in range(2, TOP_CLIP + 2):
        gain = jnp.where(kinds >= value, gain * 0.8, gain)
    gains[...] = jnp.broadcast_to(gain, gains.shape)
    keep = log_keep(decay[...])
    through = jnp.exp(frames * keep)
    state = init[...]
    for block in range(nt - 1):
        at, after = block ^ lap, (block + 1) ^ lap
        last = blocks[at, height - 1 : height, bins - 1 : bins]
        first = blocks[after, 1:2, 0:1]
        joint = jnp.where(first != last, 0.8, 1.0)
        passed = joint * (gains[at] * (through * state + blocks[at, 0:1, :]))
        state = jnp.where(block < lap, passed, state)
    tail = jnp.exp((frames - TAIL) * keep) * state + states[nf : nf + 1, :]
    for step in range(nf):
        target = own if step == 0 else messages[step - 1]
        other = here ^ step
        power = jnp.exp((other * piece).astype(f32) * keep)
        target[0:1, :] = power * state + states[pl.ds(other, 1), :]
        target[1:2, :] = tail
        target[2:3, :] = decay[...]
        if step:
            target[3:, :] = stats[...]
    previous = blocks[jnp.maximum(lap - 1, 0) ^ lap, height - 1 : height, bins - LANES : bins]
    clips_wide[:, 0:LANES] = jnp.where(lap > 0, previous, -1.0)
    for row in range(frames // bins):
        low = LANES + row * bins
        clips_wide[:, low : low + bins] = blocks[0, row + 1 : row + 2, :]


def noise_kernel(nf, place, gauss, uniform, boost, normal, first, second, boosts):
    topics, frames = gauss.shape
    piece = frames // nf
    here = place[0, 0]
    width = normal.shape[1]
    counts = wide(column(boost[...].astype(f32)), width)
    boosts[...] = counts
    normal[...] = jnp.zeros_like(normal)
    first[...] = jnp.ones_like(first)
    second[...] = jnp.ones_like(second)
    pairs = ((gauss, normal), (uniform.at[0], first), (uniform.at[1], second))
    for index in range(nf):

        @pl.when(here == index)
        def _():
            for source, target in pairs:
                target[:, 0:piece] = source[:, index * piece : (index + 1) * piece]

    for source, target in pairs:
        target[:, piece : piece + TAIL] = source[:, frames - TAIL :]
    first[...] = jnp.log(first[...])
    second[...] = jnp.where(counts >= 2.0, jnp.log(second[...]), 0.0)


def normed_kernel(nf, own, own_state, gains, *refs):
    messages, arrivals, (normed, inputs, running) = (
        refs[: nf - 1],
        refs[nf - 1 : 2 * nf - 2],
        refs[2 * nf - 2 :],
    )
    rows, bins = own.shape
    piece = rows - TAIL
    segment = piece // 8
    gain = gains[...]
    inverse = 1.0 / gain
    powers = (1 + lax.broadcasted_iota(jnp.int32, (segment, 1), 0)).astype(f32)
    normed[:, rows:, :] = jnp.zeros_like(normed[:, rows:, :])
    for step in range(nf):
        state = own_state if step == 0 else arrivals[step - 1]
        block = own if step == 0 else messages[step - 1]
        for part in range(bins // LANES):
            at = step * (bins // LANES) + part
            lanes = slice(part * LANES, (part + 1) * LANES)
            spectral = block[0:rows, lanes].astype(f32)
            rate = state[2:3, lanes]
            keep = log_keep(rate)
            fade = 1.0 - rate
            inputs[at] = spectral * inverse * rate
            total = jnp.zeros((8, LANES), f32)
            for row in range(segment):
                total = fade * total + inputs[at, pl.ds(row, 8, stride=segment), :]
                running[at, pl.ds(row, 8, stride=segment), :] = total
            carry = state[0:1, lanes]
            through = jnp.exp(segment * keep)
            fading = jnp.exp(powers * keep)
            for index in range(8):
                low = index * segment
                running[at, low : low + segment, :] += fading * carry
                carry = through * carry + total[index : index + 1, :]
            carry = state[1:2, lanes]
            for row in range(piece, rows):
                carry = fade * carry + inputs[at, row : row + 1, :]
                running[at, row : row + 1, :] = carry
            smooth = running[at] * gain
            normed[step, 0:rows, lanes] = (spectral * lax.rsqrt(smooth + 0.1)).astype(bf16)


def sampler_kernel(nf, piece, place, normed, encoder, halves, normal, first, second, boosts, *refs):
    messages, (packed, tail) = refs[: nf - 1], refs[nf - 1 :]
    core = place[0, 1] & 1
    topics, width = normal.shape
    half = topics // 2
    rows = piece + TAIL
    logits = jnp.zeros((topics, width), f32)
    for step in range(nf):
        if step == 0:
            weights = encoder[...]
        else:
            mine = messages[step - 1][rows:, :]
            other = halves[(step - 1) * half : step * half, :]
            lower = jnp.where(core == 0, mine, other)
            upper = jnp.where(core == 0, other, mine)
            weights = jnp.concatenate([lower, upper], axis=0)
        logits += lax.dot_general(
            weights, normed[step], (((1,), (1,)), ((), ())), preferred_element_type=f32
        )
    concentration = jnp.maximum(logits, 0.0) + jnp.log1p(jnp.exp(-jnp.abs(logits))) + 0.5
    offset = concentration + boosts[...] - 1.0 / 3.0
    linear = 1.0 + lax.rsqrt(9.0 * offset) * normal[...]
    draw = offset * linear * linear * linear
    draw = draw * jnp.exp(first[...] / concentration + second[...] / (concentration + 1.0))
    proportions = draw / jnp.sum(draw, axis=0, keepdims=True)
    full, rest = piece // LANES, piece % LANES
    for index in range(full):
        tile = proportions[:, index * LANES : (index + 1) * LANES]
        packed[index * topics : (index + 1) * topics, :] = tile.astype(bf16)
    tile = proportions[:, full * LANES : (full + 1) * LANES]
    if rest:
        lane = lax.broadcasted_iota(jnp.int32, (half, LANES), 1)
        joined = jnp.where(lane < rest, tile[:half], pltpu.roll(tile[half:], rest, 1))
        packed[full * topics :, :] = joined.astype(bf16)
    tail[...] = pltpu.roll(tile, LANES - TAIL - rest, 1).astype(bf16)


def rebuild_kernel(nt, nf, place, own, rim, clips, templates, spectrum, stats, *refs):
    messages, arrivals, (stacked, ratio, sums, bound), (extended, heads, recon) = (
        refs[: nf - 1],
        refs[nf - 1 : 2 * nf - 2],
        refs[2 * nf - 2 : 2 * nf + 2],
        refs[2 * nf + 2 :],
    )
    bins, frames = spectrum.shape
    here = place[0, 0]
    piece = frames // nf
    topics = extended.shape[0]
    full, rest = piece // LANES, piece % LANES
    extended[:, 0:LANES] = rim[...].astype(f32)
    for step in range(nf):
        source = own if step == 0 else messages[step - 1]
        for index in range(nf):

            @pl.when((here ^ step) == index)
            def _():
                low = LANES + index * piece
                for part in range(full):
                    values = source[part * topics : (part + 1) * topics, :].astype(f32)
                    extended[:, low + part * LANES : low + (part + 1) * LANES] = values
                if rest:
                    values = source[full * topics :, :].astype(f32)
                    low += full * LANES
                    half = topics // 2
                    extended[0:half, low : low + rest] = values[:, 0:rest]
                    extended[half:, low : low + rest] = values[:, rest:]

    total = stats[...]
    for arrival in arrivals:
        total = total + arrival[3:, :]
    columns = templates.shape[1]
    wide_rows = columns // bins
    heads[...] = jnp.zeros_like(heads)
    for row in range(wide_rows):
        value = total[row : row + 1, :]
        for index in range(3):
            rounded = value.astype(bf16)
            heads[index : index + 1, row * bins : (row + 1) * bins] = rounded
            value = value - rounded.astype(f32)
    for row in range(frames // bins):
        at = wide_rows + row
        sums[2:3, row * bins : (row + 1) * bins] = total[at : at + 1, :]
    ids = jnp.broadcast_to(clips[...], (L, LANES + frames))
    shifted = pltpu.roll(ids, 0, 1, stride=1, stride_axis=0)
    valid = jnp.where(shifted == ids, 1.0, 0.0)[:, LANES:]
    group = 32
    for low in range(0, topics, group):
        for topic in range(low, low + group):
            row = jnp.broadcast_to(extended[topic : topic + 1, :], (L, LANES + frames))
            lagged = pltpu.roll(row, 0, 1, stride=1, stride_axis=0)[:, LANES:]
            stacked[topic * L : (topic + 1) * L, :] = (lagged * valid).astype(bf16)
        part = slice(low * L, (low + group) * L)
        left = jnp.concatenate([templates[:, part], heads[:, part]], axis=0)
        product = jnp.dot(left, stacked[part, :], preferred_element_type=f32)
        if low == 0:
            recon[...] = product
        else:
            recon[...] += product
    rebuilt = recon[0:bins, :]
    recon_sum = recon[bins : bins + 1] + recon[bins + 1 : bins + 2] + recon[bins + 2 : bins + 3]
    spectral = spectrum[...].astype(f32)
    scale = F * K / (frames * nt)
    rounded = (scale * (1.0 / recon_sum - spectral / (sums[2:3, :] * rebuilt))).astype(bf16)
    turned = jnp.transpose(rounded.astype(f32))
    ratio[...] = turned.astype(bf16)
    reach = jnp.sum(jnp.abs(turned), axis=0, keepdims=True)
    bound[...] = jnp.broadcast_to(jnp.max(reach, axis=1, keepdims=True), bound.shape)
    sums[0:1, :] = recon_sum
    sums[1:2, :] = jnp.sum(spectral * jnp.log(rebuilt), axis=0, keepdims=True)


def product_kernel(side, steps, place, stacked, ratio, bound, *targets):
    height = targets[0].shape[0] - 8 * side
    lap = place[0, 1]
    for step, target in zip(steps, targets):
        at = pl.multiple_of((lap ^ (2 * step + side)) * height, height)
        target[0:height, :] = jnp.dot(
            stacked[pl.ds(at, height), :], ratio[...], preferred_element_type=f32
        )
        if side:
            target[height:, :] = bound[...]


def message_kernel(bound, kept, crossed, message):
    height = kept.shape[0]
    limit = (bound[0:1, :] + crossed[height : height + 1, :]) * (1.02 / 32768.0)
    unit = jnp.maximum(limit, 2.0**-14).astype(bf16).astype(f32)
    message[0:height, :] = (kept[...] + crossed[0:height, :]) * (1.0 / unit)
    message[height:, :] = jnp.broadcast_to(unit, (16, kept.shape[1]))


def total_kernel(kept, crossed, *refs):
    parts, total = refs[:-1], refs[-1]
    height = kept.shape[0]
    value = kept[...] + crossed[0:height, :]
    for part in parts:
        value = value + part[0:height, :] * part[height : height + 1, :]
    total[...] = value


def exchanged(value, axis, step):
    size = lax.axis_size(axis)
    return lax.ppermute(value, axis, [(index, index ^ step) for index in range(size)])


def on_device(
    spectrum,
    decay_rate,
    init_state,
    clip_ids,
    encoder,
    gauss_noise,
    uniform_noise,
    boost_count,
    templates,
):
    nt, nf = lax.axis_size("tm"), lax.axis_size("freq")
    bins, frames = spectrum.shape
    topics = encoder.shape[0]
    columns = templates.shape[1]
    piece = frames // nf
    rows = piece + TAIL
    width = -(-rows // LANES) * LANES
    place = jnp.stack([lax.axis_index("freq"), lax.axis_index("tm")]).astype(jnp.int32)[None]
    decay = decay_rate[None]
    state_rows = -(-(nf + 1) // 8) * 8
    height = 1 + frames // bins

    small = jnp.pad(decay_rate, (0, frames)) + jnp.pad(clip_ids, (bins, 0)).astype(f32)
    small = small[None]
    *messages, own, gains, states, tm_message, frame_sums = pl.pallas_call(
        functools.partial(summary_kernel, nf),
        name="summary",
        out_shape=[jax.ShapeDtypeStruct((rows + topics // 2, bins), bf16)] * (nf - 1)
        + [
            jax.ShapeDtypeStruct((rows, bins), bf16),
            jax.ShapeDtypeStruct((rows, LANES), f32),
            jax.ShapeDtypeStruct((state_rows, bins), f32),
            jax.ShapeDtypeStruct((height, bins), f32),
            jax.ShapeDtypeStruct((frames // bins, bins), f32),
        ],
        in_specs=[SMEM] + [pl.BlockSpec(memory_space=pltpu.HBM)] * 3,
        out_specs=[VMEM] * (nf + 4),
        scratch_shapes=[
            pltpu.VMEM((frames, bins), f32),
            pltpu.VMEM((bins, frames), bf16),
            pltpu.VMEM((1, bins + frames), f32),
            pltpu.VMEM((topics, bins), bf16),
            pltpu.SemaphoreType.DMA((3,)),
        ],
        compiler_params=pltpu.CompilerParams(vmem_limit_bytes=12 << 20),
    )(place, spectrum, small, encoder)
    messages = [exchanged(messages[step - 1], "freq", step) for step in range(1, nf)]
    pair = jnp.concatenate([tm_message, exchanged(tm_message, "tm", 1)], axis=0)
    pairs = [pair] + [exchanged(pair, "tm", step) for step in range(2, nt, 2)]
    stat_rows = columns // bins + frames // bins
    (stats,) = call(
        totals_kernel, "totals", [((stat_rows, bins), f32)], [], templates, frame_sums
    )
    *arrivals, own_state, clips_wide = call(
        functools.partial(entry_kernel, nt, nf),
        "entry",
        [((3 + stat_rows, bins), f32)] * (nf - 1)
        + [((3, bins), f32), ((1, LANES + frames), f32)],
        [((nt, height, bins), f32), ((nt, 1, bins), f32)],
        place,
        decay,
        init_state[None],
        states,
        stats,
        *pairs,
        scalars=1,
    )
    arrivals = [exchanged(arrivals[step - 1], "freq", step) for step in range(1, nf)]
    (halves,) = call(
        functools.partial(halves_kernel, rows),
        "halves",
        [(((nf - 1) * topics // 2, bins), bf16)],
        [],
        *arrivals,
        *messages,
    )
    halves = exchanged(halves, "tm", 1)
    noises = call(
        functools.partial(noise_kernel, nf),
        "noise",
        [((topics, width), f32)] * 4,
        [],
        place,
        gauss_noise,
        uniform_noise,
        boost_count[None],
        scalars=1,
    )
    (normed,) = call(
        functools.partial(normed_kernel, nf),
        "normed",
        [((nf, width, bins), bf16)],
        [((nf * bins // LANES, rows, LANES), f32)] * 2,
        own,
        own_state,
        gains,
        *messages,
        *arrivals,
    )
    packed, tail = call(
        functools.partial(sampler_kernel, nf, piece),
        "sampler",
        [((topics * piece // LANES, LANES), bf16), ((topics, LANES), bf16)],
        [],
        place,
        normed,
        encoder,
        halves,
        *noises,
        *messages,
        scalars=1,
    )
    shares = [exchanged(packed, "freq", step) for step in range(1, nf)]
    rim = lax.ppermute(tail, "tm", [(index, index + 1) for index in range(nt - 1)])
    stacked, ratio, sums, bound = call(
        functools.partial(rebuild_kernel, nt, nf),
        "rebuild",
        [((columns, frames), bf16), ((frames, bins), bf16), ((8, frames), f32), ((8, bins), f32)],
        [((topics, LANES + frames), f32), ((16, columns), bf16), ((bins + 16, frames), f32)],
        place,
        packed,
        rim,
        clips_wide,
        templates,
        spectrum,
        stats,
        *shares,
        *arrivals,
        scalars=1,
    )
    height = columns // nt
    order = list(range(1, nt // 2)) + [0]
    away, kept = (
        call(
            functools.partial(product_kernel, side, order),
            name,
            [((height + 8 * side, bins), f32)] * len(order),
            [],
            place,
            stacked,
            ratio,
            bound,
            scalars=1,
        )
        for side, name in ((1, "away"), (0, "kept"))
    )
    kept = dict(zip(order, kept))
    crossed = {step: exchanged(block, "tm", 1) for step, block in zip(order, away)}
    parts = []
    for step in order[:-1]:
        (message,) = call(
            message_kernel,
            "message",
            [((height + 16, bins), f32)],
            [],
            bound,
            kept[step],
            crossed[step],
        )
        part = exchanged(message.astype(jnp.float16), "tm", 2 * step)
        parts.append(part.astype(f32))
    (result,) = call(
        total_kernel, "total", [((height, bins), f32)], [], kept[0], crossed[0], *parts
    )
    log_part = sums[1]
    log_sum = log_part + sum(exchanged(log_part, "freq", step) for step in range(1, nf))
    frame_loss = jnp.log(sums[0]) - log_sum / sums[2]
    return (frame_loss, result)


def solution(mesh):
    placed = (
        P("freq", "tm"),
        P("freq"),
        P("freq"),
        P("tm"),
        P(None, "freq"),
        P(None, "tm"),
        P(None, None, "tm"),
        P(),
        P("freq", None),
    )
    return jax.shard_map(
        on_device, mesh=mesh, in_specs=placed, out_specs=(P("tm"), P("tm", "freq")), check_vma=False
    )
```

```python
import functools

import jax
import jax.numpy as jnp
from jax import lax
from jax.experimental import pallas as pl
from jax.experimental.pallas import tpu as pltpu
from jax.sharding import PartitionSpec as P

F = 1024
K = 256
L = 16
TOP_CLIP = 5
TAIL = 16
LANES = 128
VMEM = pl.BlockSpec(memory_space=pltpu.VMEM)
SMEM = pl.BlockSpec(memory_space=pltpu.SMEM)
f32 = jnp.float32
bf16 = jnp.bfloat16


def call(kernel, name, outs, scratch, *args, scalars=0, limit=12 << 20):
    return pl.pallas_call(
        kernel,
        name=name,
        out_shape=[jax.ShapeDtypeStruct(shape, dtype) for shape, dtype in outs],
        in_specs=[SMEM] * scalars + [VMEM] * (len(args) - scalars),
        out_specs=[VMEM] * len(outs),
        scratch_shapes=[pltpu.VMEM(shape, dtype) for shape, dtype in scratch],
        compiler_params=pltpu.CompilerParams(vmem_limit_bytes=limit),
        cost_estimate=pl.CostEstimate(flops=0, bytes_accessed=0, transcendentals=0),
    )(*args)


def log_keep(decay):
    gap = 1.0 - (1.0 - decay)
    series = gap * (1.0 / 7.0)
    for order in range(6, 0, -1):
        series = gap * (1.0 / order + series)
    return -series


def column(row, lanes=LANES):
    return jnp.transpose(jnp.broadcast_to(row, (lanes, row.shape[1])))


def wide(col, lanes):
    return jnp.concatenate([col] * (lanes // col.shape[1]), axis=1)


def steps_down(size):
    return (size - 1 - lax.broadcasted_iota(jnp.int32, (size, 1), 0)).astype(f32)


def pieces_kernel(nf, place, both, *refs):
    messages, (own, flipped, frame_sums, frames_first) = refs[: nf - 1], refs[nf - 1 :]
    frames, bins = flipped.shape
    spectrum, encoder = both.at[:, 0:frames], both.at[:, frames:]
    piece = frames // nf
    half = encoder.shape[0] // 2
    here, core = place[0, 0], place[0, 1] & 1
    spectral = spectrum[...].astype(f32)
    turned = jnp.transpose(spectral)
    frames_first[...] = turned
    flipped[...] = turned.astype(bf16)
    for step in range(nf):
        target = own if step == 0 else messages[step - 1]
        start = pl.multiple_of((here ^ step) * piece, piece)
        target[0:piece, :] = frames_first[pl.ds(start, piece), :].astype(bf16)
        target[piece : piece + TAIL, :] = turned[frames - TAIL :].astype(bf16)
        if step:
            low = pl.multiple_of(core * half, half)
            target[piece + TAIL :, :] = encoder[pl.ds(low, half), :]
    total = jnp.sum(spectral, axis=0, keepdims=True)
    for row in range(frames // bins):
        frame_sums[row : row + 1, :] = total[:, row * bins : (row + 1) * bins]


def summary_kernel(nf, place, flipped, small, gains, states, tm_message, all_gains):
    frames, bins = flipped.shape
    piece = frames // nf
    here = place[0, 0]
    clip_row = small[:, bins:]
    clip_col = column(clip_row)
    first = clip_row[:, :1]
    gain = jnp.ones_like(clip_col)
    for value in range(1, TOP_CLIP + 1):
        seen = jnp.max(jnp.where(clip_row == value, 1.0, 0.0), axis=1, keepdims=True)
        counts = (seen > 0.0) & (first < value)
        gain = jnp.where(counts & (clip_col >= value), gain * 0.8, gain)
    all_gains[...] = gain
    start = pl.multiple_of(here * piece, piece)
    gains[0:piece, :] = all_gains[pl.ds(start, piece), :]
    gains[piece:, :] = gain[frames - TAIL :]
    rate = small[:, 0:bins]
    keep = log_keep(rate)
    scaled = flipped[...].astype(f32) * wide(1.0 / gain, bins) * rate
    weights = jnp.exp(steps_down(piece) * keep)
    state = jnp.zeros((1, bins), f32)
    states[...] = jnp.zeros_like(states)
    for index in range(nf):
        states[index : index + 1, :] = state
        rows = scaled[index * piece : (index + 1) * piece]
        if index < nf - 1:
            state = jnp.exp(piece * keep) * state + jnp.sum(rows * weights, axis=0, keepdims=True)
    body = piece - TAIL
    state = jnp.exp(body * keep) * state + jnp.sum(
        rows[:body] * weights[TAIL:], axis=0, keepdims=True
    )
    states[nf : nf + 1, :] = state
    state = jnp.exp(TAIL * keep) * state + jnp.sum(
        rows[body:] * weights[body:], axis=0, keepdims=True
    )
    tm_message[0:1, :] = state
    for row in range(frames // bins):
        tm_message[row + 1 : row + 2, :] = clip_row[:, row * bins : (row + 1) * bins]


def halves_kernel(rows, _, *refs):
    messages = refs[len(refs) // 2 : -1]
    half = messages[0].shape[0] - rows
    for index, message in enumerate(messages):
        refs[-1][index * half : (index + 1) * half, :] = message[rows:, :]


def totals_kernel(templates, frame_sums, stats):
    bins, columns = templates.shape
    for row in range(columns // bins):
        part = templates[:, row * bins : (row + 1) * bins].astype(f32)
        stats[row : row + 1, :] = jnp.sum(part, axis=0, keepdims=True)
    stats[columns // bins : columns // bins + frame_sums.shape[0], :] = frame_sums[...]


def entry_kernel(nt, nf, place, decay, init, states, stats, *refs):
    refs = refs[nf - 2 :]
    pairs, messages, (own, clips_wide), (blocks, gains) = (
        refs[: nt // 2],
        refs[nt // 2 : nt // 2 + nf - 1],
        refs[nt // 2 + nf - 1 : nt // 2 + nf + 1],
        refs[nt // 2 + nf + 1 :],
    )
    bins = decay.shape[1]
    height = blocks.shape[1]
    frames = (height - 1) * bins
    piece = frames // nf
    here, lap = place[0, 0], place[0, 1]
    for index, pair in enumerate(pairs):
        blocks[2 * index] = pair[0:height]
        blocks[2 * index + 1] = pair[height:]
    ids = blocks[:, 1:, :]
    kinds = jnp.zeros((nt, 1, 1), f32)
    for value in range(TOP_CLIP + 1):
        kinds += jnp.max(jnp.where(ids == value, 1.0, 0.0), axis=(1, 2), keepdims=True)
    gain = jnp.ones_like(kinds)
    for value in range(2, TOP_CLIP + 2):
        gain = jnp.where(kinds >= value, gain * 0.8, gain)
    gains[...] = jnp.broadcast_to(gain, gains.shape)
    keep = log_keep(decay[...])
    through = jnp.exp(frames * keep)
    state = init[...]
    for block in range(nt - 1):
        at, after = block ^ lap, (block + 1) ^ lap
        last = blocks[at, height - 1 : height, bins - 1 : bins]
        first = blocks[after, 1:2, 0:1]
        joint = jnp.where(first != last, 0.8, 1.0)
        passed = joint * (gains[at] * (through * state + blocks[at, 0:1, :]))
        state = jnp.where(block < lap, passed, state)
    tail = jnp.exp((frames - TAIL) * keep) * state + states[nf : nf + 1, :]
    for step in range(nf):
        target = own if step == 0 else messages[step - 1]
        other = here ^ step
        power = jnp.exp((other * piece).astype(f32) * keep)
        target[0:1, :] = power * state + states[pl.ds(other, 1), :]
        target[1:2, :] = tail
        target[2:3, :] = decay[...]
        if step:
            target[3:, :] = stats[...]
    previous = blocks[jnp.maximum(lap - 1, 0) ^ lap, height - 1 : height, bins - LANES : bins]
    clips_wide[:, 0:LANES] = jnp.where(lap > 0, previous, -1.0)
    for row in range(frames // bins):
        low = LANES + row * bins
        clips_wide[:, low : low + bins] = blocks[0, row + 1 : row + 2, :]


def noise_kernel(nf, place, gauss, uniform, boost, normal, first, second, boosts):
    topics, frames = gauss.shape
    piece = frames // nf
    here = place[0, 0]
    width = normal.shape[1]
    counts = wide(column(boost[...].astype(f32)), width)
    boosts[...] = counts
    normal[...] = jnp.zeros_like(normal)
    first[...] = jnp.ones_like(first)
    second[...] = jnp.ones_like(second)
    pairs = ((gauss, normal), (uniform.at[0], first), (uniform.at[1], second))
    for index in range(nf):

        @pl.when(here == index)
        def _():
            for source, target in pairs:
                target[:, 0:piece] = source[:, index * piece : (index + 1) * piece]

    for source, target in pairs:
        target[:, piece : piece + TAIL] = source[:, frames - TAIL :]
    first[...] = jnp.log(first[...])
    second[...] = jnp.where(counts >= 2.0, jnp.log(second[...]), 0.0)


def normed_kernel(nf, own, own_state, gains, *refs):
    messages, arrivals, (normed, inputs, running) = (
        refs[: nf - 1],
        refs[nf - 1 : 2 * nf - 2],
        refs[2 * nf - 2 :],
    )
    rows, bins = own.shape
    piece = rows - TAIL
    segment = piece // 8
    gain = gains[...]
    inverse = 1.0 / gain
    powers = (1 + lax.broadcasted_iota(jnp.int32, (segment, 1), 0)).astype(f32)
    normed[:, rows:, :] = jnp.zeros_like(normed[:, rows:, :])
    for step in range(nf):
        state = own_state if step == 0 else arrivals[step - 1]
        block = own if step == 0 else messages[step - 1]
        for part in range(bins // LANES):
            at = step * (bins // LANES) + part
            lanes = slice(part * LANES, (part + 1) * LANES)
            spectral = block[0:rows, lanes].astype(f32)
            rate = state[2:3, lanes]
            keep = log_keep(rate)
            fade = 1.0 - rate
            inputs[at] = spectral * inverse * rate
            total = jnp.zeros((8, LANES), f32)
            for row in range(segment):
                total = fade * total + inputs[at, pl.ds(row, 8, stride=segment), :]
                running[at, pl.ds(row, 8, stride=segment), :] = total
            carry = state[0:1, lanes]
            through = jnp.exp(segment * keep)
            fading = jnp.exp(powers * keep)
            for index in range(8):
                low = index * segment
                running[at, low : low + segment, :] += fading * carry
                carry = through * carry + total[index : index + 1, :]
            carry = state[1:2, lanes]
            for row in range(piece, rows):
                carry = fade * carry + inputs[at, row : row + 1, :]
                running[at, row : row + 1, :] = carry
            smooth = running[at] * gain
            normed[step, 0:rows, lanes] = (spectral * lax.rsqrt(smooth + 0.1)).astype(bf16)


def sampler_kernel(nf, piece, place, normed, encoder, halves, normal, first, second, boosts, *refs):
    messages, (packed, tail) = refs[: nf - 1], refs[nf - 1 :]
    core = place[0, 1] & 1
    topics, width = normal.shape
    half = topics // 2
    rows = piece + TAIL
    logits = jnp.zeros((topics, width), f32)
    for step in range(nf):
        if step == 0:
            weights = encoder[...]
        else:
            mine = messages[step - 1][rows:, :]
            other = halves[(step - 1) * half : step * half, :]
            lower = jnp.where(core == 0, mine, other)
            upper = jnp.where(core == 0, other, mine)
            weights = jnp.concatenate([lower, upper], axis=0)
        logits += lax.dot_general(
            weights, normed[step], (((1,), (1,)), ((), ())), preferred_element_type=f32
        )
    concentration = jnp.maximum(logits, 0.0) + jnp.log1p(jnp.exp(-jnp.abs(logits))) + 0.5
    offset = concentration + boosts[...] - 1.0 / 3.0
    linear = 1.0 + lax.rsqrt(9.0 * offset) * normal[...]
    draw = offset * linear * linear * linear
    draw = draw * jnp.exp(first[...] / concentration + second[...] / (concentration + 1.0))
    proportions = draw / jnp.sum(draw, axis=0, keepdims=True)
    full, rest = piece // LANES, piece % LANES
    for index in range(full):
        tile = proportions[:, index * LANES : (index + 1) * LANES]
        packed[index * topics : (index + 1) * topics, :] = tile.astype(bf16)
    tile = proportions[:, full * LANES : (full + 1) * LANES]
    if rest:
        lane = lax.broadcasted_iota(jnp.int32, (half, LANES), 1)
        joined = jnp.where(lane < rest, tile[:half], pltpu.roll(tile[half:], rest, 1))
        packed[full * topics :, :] = joined.astype(bf16)
    tail[...] = pltpu.roll(tile, LANES - TAIL - rest, 1).astype(bf16)


def rebuild_kernel(nt, nf, place, own, rim, clips, templates, spectrum, stats, *refs):
    messages, arrivals, (stacked, ratio, sums, bound), (extended, heads, recon) = (
        refs[: nf - 1],
        refs[nf - 1 : 2 * nf - 2],
        refs[2 * nf - 2 : 2 * nf + 2],
        refs[2 * nf + 2 :],
    )
    bins, frames = spectrum.shape
    here = place[0, 0]
    piece = frames // nf
    topics = extended.shape[0]
    full, rest = piece // LANES, piece % LANES
    extended[:, 0:LANES] = rim[...].astype(f32)
    for step in range(nf):
        source = own if step == 0 else messages[step - 1]
        for index in range(nf):

            @pl.when((here ^ step) == index)
            def _():
                low = LANES + index * piece
                for part in range(full):
                    values = source[part * topics : (part + 1) * topics, :].astype(f32)
                    extended[:, low + part * LANES : low + (part + 1) * LANES] = values
                if rest:
                    values = source[full * topics :, :].astype(f32)
                    low += full * LANES
                    half = topics // 2
                    extended[0:half, low : low + rest] = values[:, 0:rest]
                    extended[half:, low : low + rest] = values[:, rest:]

    total = stats[...]
    for arrival in arrivals:
        total = total + arrival[3:, :]
    columns = templates.shape[1]
    wide_rows = columns // bins
    heads[...] = jnp.zeros_like(heads)
    for row in range(wide_rows):
        value = total[row : row + 1, :]
        for index in range(3):
            rounded = value.astype(bf16)
            heads[index : index + 1, row * bins : (row + 1) * bins] = rounded
            value = value - rounded.astype(f32)
    for row in range(frames // bins):
        at = wide_rows + row
        sums[2:3, row * bins : (row + 1) * bins] = total[at : at + 1, :]
    ids = jnp.broadcast_to(clips[...], (L, LANES + frames))
    shifted = pltpu.roll(ids, 0, 1, stride=1, stride_axis=0)
    valid = jnp.where(shifted == ids, 1.0, 0.0)[:, LANES:]
    group = 32
    for low in range(0, topics, group):
        for topic in range(low, low + group):
            row = jnp.broadcast_to(extended[topic : topic + 1, :], (L, LANES + frames))
            lagged = pltpu.roll(row, 0, 1, stride=1, stride_axis=0)[:, LANES:]
            stacked[topic * L : (topic + 1) * L, :] = (lagged * valid).astype(bf16)
        part = slice(low * L, (low + group) * L)
        left = jnp.concatenate([templates[:, part], heads[:, part]], axis=0)
        product = jnp.dot(left, stacked[part, :], preferred_element_type=f32)
        if low == 0:
            recon[...] = product
        else:
            recon[...] += product
    rebuilt = recon[0:bins, :]
    recon_sum = recon[bins : bins + 1] + recon[bins + 1 : bins + 2] + recon[bins + 2 : bins + 3]
    spectral = spectrum[...].astype(f32)
    scale = F * K / (frames * nt)
    rounded = (scale * (1.0 / recon_sum - spectral / (sums[2:3, :] * rebuilt))).astype(bf16)
    turned = jnp.transpose(rounded.astype(f32))
    ratio[...] = turned.astype(bf16)
    reach = jnp.sum(jnp.abs(turned), axis=0, keepdims=True)
    bound[...] = jnp.broadcast_to(jnp.max(reach, axis=1, keepdims=True), bound.shape)
    sums[0:1, :] = recon_sum
    sums[1:2, :] = jnp.sum(spectral * jnp.log(rebuilt), axis=0, keepdims=True)


def product_kernel(side, routed, place, stacked, ratio, bound, *targets):
    height = targets[0].shape[0] - 8 * side
    lap = place[0, 1]
    hop = 1 + ((lap ^ side) & 1)
    order = (3, hop, 3 ^ hop, 0) if routed else (*range(1, len(targets)), 0)
    for step, target in zip(order, targets):
        at = pl.multiple_of((lap ^ (2 * step + side)) * height, height)
        target[0:height, :] = jnp.dot(
            stacked[pl.ds(at, height), :], ratio[...], preferred_element_type=f32
        )
        if side:
            target[height:, :] = bound[...]


def message_kernel(bound, kept, crossed, *refs):
    parts, message = refs[:-1], refs[-1]
    height = kept.shape[0]
    limit = bound[0:1, :] + crossed[height : height + 1, :]
    value = kept[...] + crossed[0:height, :]
    for part in parts:
        carried = part[height : height + 1, :]
        limit = limit + carried * 32768.0
        value = value + part[0:height, :] * carried
    unit = jnp.maximum(limit * (1.02 / 32768.0), 2.0**-14).astype(bf16).astype(f32)
    message[0:height, :] = value * (1.0 / unit)
    message[height:, :] = jnp.broadcast_to(unit, (16, kept.shape[1]))


def total_kernel(kept, crossed, *refs):
    parts, total = refs[:-1], refs[-1]
    height = kept.shape[0]
    value = kept[...] + crossed[0:height, :]
    for part in parts:
        value = value + part[0:height, :] * part[height : height + 1, :]
    total[...] = value


def exchanged(value, axis, step):
    size = lax.axis_size(axis)
    return lax.ppermute(value, axis, [(index, index ^ step) for index in range(size)])


def on_device(
    spectrum,
    decay_rate,
    init_state,
    clip_ids,
    encoder,
    gauss_noise,
    uniform_noise,
    boost_count,
    templates,
):
    nt, nf = lax.axis_size("tm"), lax.axis_size("freq")
    bins, frames = spectrum.shape
    topics = encoder.shape[0]
    columns = templates.shape[1]
    piece = frames // nf
    rows = piece + TAIL
    width = -(-rows // LANES) * LANES
    place = jnp.stack([lax.axis_index("freq"), lax.axis_index("tm")]).astype(jnp.int32)[None]
    decay = decay_rate[None]
    state_rows = -(-(nf + 1) // 8) * 8
    height = 1 + frames // bins

    *messages, own, flipped, frame_sums = call(
        functools.partial(pieces_kernel, nf),
        "pieces",
        [((rows + topics // 2, bins), bf16)] * (nf - 1)
        + [((rows, bins), bf16), ((frames, bins), bf16), ((frames // bins, bins), f32)],
        [((frames, bins), f32)],
        place,
        jnp.concatenate([spectrum, encoder], axis=1),
        scalars=1,
    )
    small = jnp.pad(decay_rate, (0, frames)) + jnp.pad(clip_ids, (bins, 0)).astype(f32)
    gains, states, tm_message = call(
        functools.partial(summary_kernel, nf),
        "summary",
        [((rows, LANES), f32), ((state_rows, bins), f32), ((height, bins), f32)],
        [((frames, LANES), f32)],
        place,
        flipped,
        small[None],
        scalars=1,
    )
    messages = [exchanged(messages[step - 1], "freq", step) for step in range(1, nf)]
    pair = jnp.concatenate([tm_message, exchanged(tm_message, "tm", 1)], axis=0)
    pairs = [pair] + [exchanged(pair, "tm", step) for step in range(2, nt, 2)]
    stat_rows = columns // bins + frames // bins
    (stats,) = call(
        totals_kernel, "totals", [((stat_rows, bins), f32)], [], templates, frame_sums
    )
    *arrivals, own_state, clips_wide = call(
        functools.partial(entry_kernel, nt, nf),
        "entry",
        [((3 + stat_rows, bins), f32)] * (nf - 1)
        + [((3, bins), f32), ((1, LANES + frames), f32)],
        [((nt, height, bins), f32), ((nt, 1, bins), f32)],
        place,
        decay,
        init_state[None],
        states,
        stats,
        *messages[: nf - 2],
        *pairs,
        scalars=1,
    )
    arrivals = [exchanged(arrivals[step - 1], "freq", step) for step in range(1, nf)]
    noises = call(
        functools.partial(noise_kernel, nf),
        "noise",
        [((topics, width), f32)] * 4,
        [],
        place,
        gauss_noise,
        uniform_noise,
        boost_count[None],
        scalars=1,
    )
    (halves,) = call(
        functools.partial(halves_kernel, rows),
        "halves",
        [(((nf - 1) * topics // 2, bins), bf16)],
        [],
        noises[0],
        *arrivals,
        *messages,
    )
    halves = exchanged(halves, "tm", 1)
    (normed,) = call(
        functools.partial(normed_kernel, nf),
        "normed",
        [((nf, width, bins), bf16)],
        [((nf * bins // LANES, rows, LANES), f32)] * 2,
        own,
        own_state,
        gains,
        *messages,
        *arrivals,
    )
    packed, tail = call(
        functools.partial(sampler_kernel, nf, piece),
        "sampler",
        [((topics * piece // LANES, LANES), bf16), ((topics, LANES), bf16)],
        [],
        place,
        normed,
        encoder,
        halves,
        *noises,
        *messages,
        scalars=1,
    )
    shares = [exchanged(packed, "freq", step) for step in range(1, nf)]
    rim = lax.ppermute(tail, "tm", [(index, index + 1) for index in range(nt - 1)])
    stacked, ratio, sums, bound = call(
        functools.partial(rebuild_kernel, nt, nf),
        "rebuild",
        [((columns, frames), bf16), ((frames, bins), bf16), ((8, frames), f32), ((8, bins), f32)],
        [((topics, LANES + frames), f32), ((16, columns), bf16), ((bins + 16, frames), f32)],
        place,
        packed,
        rim,
        clips_wide,
        templates,
        spectrum,
        stats,
        *shares,
        *arrivals,
        scalars=1,
    )
    height = columns // nt
    routed = nt == 8
    steps = [1 << power for power in range(nf.bit_length() - 1)]
    log_sum = sums[1:2] + exchanged(sums[1:2], "freq", steps[0])
    away, kept = (
        call(
            functools.partial(product_kernel, side, routed),
            name,
            [((height + 8 * side, bins), f32)] * (nt // 2),
            [],
            place,
            stacked,
            ratio,
            bound,
            scalars=1,
        )
        for side, name in ((1, "away"), (0, "kept"))
    )
    crossed = [exchanged(block, "tm", 1) for block in away]

    def sent(index, pairs, *extra):
        (message,) = call(
            message_kernel,
            "message",
            [((height + 16, bins), f32)],
            [],
            bound,
            kept[index],
            crossed[index],
            *extra,
        )
        return lax.ppermute(message.astype(jnp.float16), "tm", pairs).astype(f32)

    if routed:
        first = [(lap, lap ^ (2 << (lap & 1))) for lap in range(nt)]
        second = [(lap, lap ^ (4 >> (lap & 1))) for lap in range(nt)]
        carried = sent(0, first)
        carried, log_sum = lax.optimization_barrier((carried, log_sum))
        parts = [sent(1, first), sent(2, second, carried)]
    else:
        parts = [
            sent(step - 1, [(lap, lap ^ (2 * step)) for lap in range(nt)])
            for step in range(1, nt // 2)
        ]
    (result,) = call(
        total_kernel, "total", [((height, bins), f32)], [], kept[-1], crossed[-1], *parts
    )
    for step in steps[1:]:
        log_sum = log_sum + exchanged(log_sum, "freq", step)
    frame_loss = jnp.log(sums[0]) - log_sum[0] / sums[2]
    return (frame_loss, result)


def solution(mesh):
    placed = (
        P("freq", "tm"),
        P("freq"),
        P("freq"),
        P("tm"),
        P(None, "freq"),
        P(None, "tm"),
        P(None, None, "tm"),
        P(),
        P("freq", None),
    )
    return jax.shard_map(
        on_device, mesh=mesh, in_specs=placed, out_specs=(P("tm"), P("tm", "freq")), check_vma=False
    )
```

```python
import functools

import jax
import jax.numpy as jnp
from jax import lax
from jax.experimental import pallas as pl
from jax.experimental.pallas import tpu as pltpu
from jax.sharding import PartitionSpec as P

F = 1024
K = 256
L = 16
TOP_CLIP = 5
TAIL = 16
LANES = 128
VMEM = pl.BlockSpec(memory_space=pltpu.VMEM)
SMEM = pl.BlockSpec(memory_space=pltpu.SMEM)
f32 = jnp.float32
bf16 = jnp.bfloat16


def call(kernel, name, outs, scratch, *args, scalars=0, limit=12 << 20):
    return pl.pallas_call(
        kernel,
        name=name,
        out_shape=[jax.ShapeDtypeStruct(shape, dtype) for shape, dtype in outs],
        in_specs=[SMEM] * scalars + [VMEM] * (len(args) - scalars),
        out_specs=[VMEM] * len(outs),
        scratch_shapes=[pltpu.VMEM(shape, dtype) for shape, dtype in scratch],
        compiler_params=pltpu.CompilerParams(vmem_limit_bytes=limit),
        cost_estimate=pl.CostEstimate(flops=0, bytes_accessed=0, transcendentals=0),
    )(*args)


def log_keep(decay):
    gap = 1.0 - (1.0 - decay)
    series = gap * (1.0 / 7.0)
    for order in range(6, 0, -1):
        series = gap * (1.0 / order + series)
    return -series


def column(row, lanes=LANES):
    return jnp.transpose(jnp.broadcast_to(row, (lanes, row.shape[1])))


def wide(col, lanes):
    return jnp.concatenate([col] * (lanes // col.shape[1]), axis=1)


def steps_down(size):
    return (size - 1 - lax.broadcasted_iota(jnp.int32, (size, 1), 0)).astype(f32)


def pieces_kernel(nf, place, both, *refs):
    messages, (own, flipped, frame_sums, frames_first) = refs[: nf - 1], refs[nf - 1 :]
    frames, bins = flipped.shape
    spectrum, encoder = both.at[:, 0:frames], both.at[:, frames:]
    piece = frames // nf
    half = encoder.shape[0] // 2
    here, core = place[0, 0], place[0, 1] & 1
    spectral = spectrum[...].astype(f32)
    turned = jnp.transpose(spectral)
    frames_first[...] = turned
    flipped[...] = turned.astype(bf16)
    for step in range(nf):
        target = own if step == 0 else messages[-step]
        start = pl.multiple_of((here ^ step) * piece, piece)
        target[0:piece, :] = frames_first[pl.ds(start, piece), :].astype(bf16)
        target[piece : piece + TAIL, :] = turned[frames - TAIL :].astype(bf16)
        if step:
            low = pl.multiple_of(core * half, half)
            target[piece + TAIL :, :] = encoder[pl.ds(low, half), :]
    total = jnp.sum(spectral, axis=0, keepdims=True)
    for row in range(frames // bins):
        frame_sums[row : row + 1, :] = total[:, row * bins : (row + 1) * bins]


def summary_kernel(nf, place, flipped, small, gains, states, tm_message, all_gains):
    frames, bins = flipped.shape
    piece = frames // nf
    here = place[0, 0]
    clip_row = small[:, bins:]
    clip_col = column(clip_row)
    first = clip_row[:, :1]
    gain = jnp.ones_like(clip_col)
    for value in range(1, TOP_CLIP + 1):
        seen = jnp.max(jnp.where(clip_row == value, 1.0, 0.0), axis=1, keepdims=True)
        counts = (seen > 0.0) & (first < value)
        gain = jnp.where(counts & (clip_col >= value), gain * 0.8, gain)
    all_gains[...] = gain
    start = pl.multiple_of(here * piece, piece)
    gains[0:piece, :] = all_gains[pl.ds(start, piece), :]
    gains[piece:, :] = gain[frames - TAIL :]
    rate = small[:, 0:bins]
    keep = log_keep(rate)
    scaled = flipped[...].astype(f32) * wide(1.0 / gain, bins) * rate
    weights = jnp.exp(steps_down(piece) * keep)
    state = jnp.zeros((1, bins), f32)
    states[...] = jnp.zeros_like(states)
    for index in range(nf):
        states[index : index + 1, :] = state
        rows = scaled[index * piece : (index + 1) * piece]
        if index < nf - 1:
            state = jnp.exp(piece * keep) * state + jnp.sum(rows * weights, axis=0, keepdims=True)
    body = piece - TAIL
    state = jnp.exp(body * keep) * state + jnp.sum(
        rows[:body] * weights[TAIL:], axis=0, keepdims=True
    )
    states[nf : nf + 1, :] = state
    state = jnp.exp(TAIL * keep) * state + jnp.sum(
        rows[body:] * weights[body:], axis=0, keepdims=True
    )
    tm_message[0:1, :] = state
    for row in range(frames // bins):
        tm_message[row + 1 : row + 2, :] = clip_row[:, row * bins : (row + 1) * bins]


def halves_kernel(rows, _, *refs):
    messages = refs[len(refs) // 2 : -1]
    half = messages[0].shape[0] - rows
    for index, message in enumerate(messages):
        refs[-1][index * half : (index + 1) * half, :] = message[rows:, :]


def totals_kernel(templates, frame_sums, stats):
    bins, columns = templates.shape
    for row in range(columns // bins):
        part = templates[:, row * bins : (row + 1) * bins].astype(f32)
        stats[row : row + 1, :] = jnp.sum(part, axis=0, keepdims=True)
    stats[columns // bins : columns // bins + frame_sums.shape[0], :] = frame_sums[...]


def entry_kernel(nt, nf, place, decay, init, states, stats, *refs):
    refs = refs[1:]
    pairs, messages, (own, clips_wide), (blocks, gains) = (
        refs[: nt // 2],
        refs[nt // 2 : nt // 2 + nf - 1],
        refs[nt // 2 + nf - 1 : nt // 2 + nf + 1],
        refs[nt // 2 + nf + 1 :],
    )
    bins = decay.shape[1]
    height = blocks.shape[1]
    frames = (height - 1) * bins
    piece = frames // nf
    here, lap = place[0, 0], place[0, 1]
    for index, pair in enumerate(pairs):
        blocks[2 * index] = pair[0:height]
        blocks[2 * index + 1] = pair[height:]
    ids = blocks[:, 1:, :]
    kinds = jnp.zeros((nt, 1, 1), f32)
    for value in range(TOP_CLIP + 1):
        kinds += jnp.max(jnp.where(ids == value, 1.0, 0.0), axis=(1, 2), keepdims=True)
    gain = jnp.ones_like(kinds)
    for value in range(2, TOP_CLIP + 2):
        gain = jnp.where(kinds >= value, gain * 0.8, gain)
    gains[...] = jnp.broadcast_to(gain, gains.shape)
    keep = log_keep(decay[...])
    through = jnp.exp(frames * keep)
    state = init[...]
    for block in range(nt - 1):
        at, after = block ^ lap, (block + 1) ^ lap
        last = blocks[at, height - 1 : height, bins - 1 : bins]
        first = blocks[after, 1:2, 0:1]
        joint = jnp.where(first != last, 0.8, 1.0)
        passed = joint * (gains[at] * (through * state + blocks[at, 0:1, :]))
        state = jnp.where(block < lap, passed, state)
    tail = jnp.exp((frames - TAIL) * keep) * state + states[nf : nf + 1, :]
    for step in range(nf):
        target = own if step == 0 else messages[-step]
        other = here ^ step
        power = jnp.exp((other * piece).astype(f32) * keep)
        target[0:1, :] = power * state + states[pl.ds(other, 1), :]
        target[1:2, :] = tail
        target[2:3, :] = decay[...]
        if step:
            target[3:, :] = stats[...]
    previous = blocks[jnp.maximum(lap - 1, 0) ^ lap, height - 1 : height, bins - LANES : bins]
    clips_wide[:, 0:LANES] = jnp.where(lap > 0, previous, -1.0)
    for row in range(frames // bins):
        low = LANES + row * bins
        clips_wide[:, low : low + bins] = blocks[0, row + 1 : row + 2, :]


def noise_kernel(nf, place, gauss, uniform, boost, normal, first, second, boosts):
    topics, frames = gauss.shape
    piece = frames // nf
    here = place[0, 0]
    width = normal.shape[1]
    counts = wide(column(boost[...].astype(f32)), width)
    boosts[...] = counts
    normal[...] = jnp.zeros_like(normal)
    first[...] = jnp.ones_like(first)
    second[...] = jnp.ones_like(second)
    pairs = ((gauss, normal), (uniform.at[0], first), (uniform.at[1], second))
    for index in range(nf):

        @pl.when(here == index)
        def _():
            for source, target in pairs:
                target[:, 0:piece] = source[:, index * piece : (index + 1) * piece]

    for source, target in pairs:
        target[:, piece : piece + TAIL] = source[:, frames - TAIL :]
    first[...] = jnp.log(first[...])
    second[...] = jnp.where(counts >= 2.0, jnp.log(second[...]), 0.0)


def normed_kernel(nf, own, own_state, gains, *refs):
    messages, arrivals, (normed, inputs, running) = (
        refs[: nf - 1],
        refs[nf - 1 : 2 * nf - 2],
        refs[2 * nf - 2 :],
    )
    rows, bins = own.shape
    piece = rows - TAIL
    segment = piece // 8
    gain = gains[...]
    inverse = 1.0 / gain
    powers = (1 + lax.broadcasted_iota(jnp.int32, (segment, 1), 0)).astype(f32)
    normed[:, rows:, :] = jnp.zeros_like(normed[:, rows:, :])
    for step in range(nf):
        state = own_state if step == 0 else arrivals[-step]
        block = own if step == 0 else messages[-step]
        for part in range(bins // LANES):
            at = step * (bins // LANES) + part
            lanes = slice(part * LANES, (part + 1) * LANES)
            spectral = block[0:rows, lanes].astype(f32)
            rate = state[2:3, lanes]
            keep = log_keep(rate)
            fade = 1.0 - rate
            inputs[at] = spectral * inverse * rate
            total = jnp.zeros((8, LANES), f32)
            for row in range(segment):
                total = fade * total + inputs[at, pl.ds(row, 8, stride=segment), :]
                running[at, pl.ds(row, 8, stride=segment), :] = total
            carry = state[0:1, lanes]
            through = jnp.exp(segment * keep)
            fading = jnp.exp(powers * keep)
            for index in range(8):
                low = index * segment
                running[at, low : low + segment, :] += fading * carry
                carry = through * carry + total[index : index + 1, :]
            carry = state[1:2, lanes]
            for row in range(piece, rows):
                carry = fade * carry + inputs[at, row : row + 1, :]
                running[at, row : row + 1, :] = carry
            smooth = running[at] * gain
            normed[step, 0:rows, lanes] = (spectral * lax.rsqrt(smooth + 0.1)).astype(bf16)


def sampler_kernel(nf, piece, place, normed, encoder, halves, normal, first, second, boosts, *refs):
    messages, (packed, tail) = refs[: nf - 1], refs[nf - 1 :]
    core = place[0, 1] & 1
    topics, width = normal.shape
    half = topics // 2
    rows = piece + TAIL
    logits = jnp.zeros((topics, width), f32)
    for step in range(nf):
        if step == 0:
            weights = encoder[...]
        else:
            mine = messages[-step][rows:, :]
            other = halves[(nf - 1 - step) * half : (nf - step) * half, :]
            lower = jnp.where(core == 0, mine, other)
            upper = jnp.where(core == 0, other, mine)
            weights = jnp.concatenate([lower, upper], axis=0)
        logits += lax.dot_general(
            weights, normed[step], (((1,), (1,)), ((), ())), preferred_element_type=f32
        )
    concentration = jnp.maximum(logits, 0.0) + jnp.log1p(jnp.exp(-jnp.abs(logits))) + 0.5
    offset = concentration + boosts[...] - 1.0 / 3.0
    linear = 1.0 + lax.rsqrt(9.0 * offset) * normal[...]
    draw = offset * linear * linear * linear
    draw = draw * jnp.exp(first[...] / concentration + second[...] / (concentration + 1.0))
    proportions = draw / jnp.sum(draw, axis=0, keepdims=True)
    full, rest = piece // LANES, piece % LANES
    for index in range(full):
        tile = proportions[:, index * LANES : (index + 1) * LANES]
        packed[index * topics : (index + 1) * topics, :] = tile.astype(bf16)
    tile = proportions[:, full * LANES : (full + 1) * LANES]
    if rest:
        lane = lax.broadcasted_iota(jnp.int32, (half, LANES), 1)
        joined = jnp.where(lane < rest, tile[:half], pltpu.roll(tile[half:], rest, 1))
        packed[full * topics :, :] = joined.astype(bf16)
    tail[...] = pltpu.roll(tile, LANES - TAIL - rest, 1).astype(bf16)


def rebuild_kernel(nt, nf, place, own, rim, clips, templates, spectrum, stats, *refs):
    messages, arrivals, (stacked, ratio, sums, bound, *away, extended, heads, recon) = (
        refs[: nf - 1],
        refs[nf - 1 : 2 * nf - 2],
        refs[2 * nf - 2 :],
    )
    bins, frames = spectrum.shape
    here = place[0, 0]
    piece = frames // nf
    topics = extended.shape[0]
    full, rest = piece // LANES, piece % LANES
    extended[:, 0:LANES] = rim[...].astype(f32)
    for step in range(nf):
        source = own if step == 0 else messages[-step]
        for index in range(nf):

            @pl.when((here ^ step) == index)
            def _():
                low = LANES + index * piece
                for part in range(full):
                    values = source[part * topics : (part + 1) * topics, :].astype(f32)
                    extended[:, low + part * LANES : low + (part + 1) * LANES] = values
                if rest:
                    values = source[full * topics :, :].astype(f32)
                    low += full * LANES
                    half = topics // 2
                    extended[0:half, low : low + rest] = values[:, 0:rest]
                    extended[half:, low : low + rest] = values[:, rest:]

    total = stats[...]
    for arrival in arrivals:
        total = total + arrival[3:, :]
    columns = templates.shape[1]
    wide_rows = columns // bins
    heads[...] = jnp.zeros_like(heads)
    for row in range(wide_rows):
        value = total[row : row + 1, :]
        for index in range(3):
            rounded = value.astype(bf16)
            heads[index : index + 1, row * bins : (row + 1) * bins] = rounded
            value = value - rounded.astype(f32)
    for row in range(frames // bins):
        at = wide_rows + row
        sums[2:3, row * bins : (row + 1) * bins] = total[at : at + 1, :]
    ids = jnp.broadcast_to(clips[...], (L, LANES + frames))
    shifted = pltpu.roll(ids, 0, 1, stride=1, stride_axis=0)
    valid = jnp.where(shifted == ids, 1.0, 0.0)[:, LANES:].astype(bf16)
    group = 32
    for low in range(0, topics, group):
        for topic in range(low, low + group):
            row = jnp.broadcast_to(extended[topic : topic + 1, :], (L, LANES + frames))
            lagged = pltpu.roll(row, 0, 1, stride=1, stride_axis=0)[:, LANES:]
            stacked[topic * L : (topic + 1) * L, :] = lagged.astype(bf16) * valid
        part = slice(low * L, (low + group) * L)
        left = jnp.concatenate([templates[:, part], heads[:, part]], axis=0)
        product = jnp.dot(left, stacked[part, :], preferred_element_type=f32)
        if low == 0:
            recon[...] = product
        else:
            recon[...] += product
    rebuilt = recon[0:bins, :]
    recon_sum = recon[bins : bins + 1] + recon[bins + 1 : bins + 2] + recon[bins + 2 : bins + 3]
    spectral = spectrum[...].astype(f32)
    scale = F * K / (frames * nt)
    rounded = (scale * (1.0 / recon_sum - spectral / (sums[2:3, :] * rebuilt))).astype(bf16)
    turned = jnp.transpose(rounded.astype(f32))
    ratio[...] = turned.astype(bf16)
    reach = jnp.sum(jnp.abs(turned), axis=0, keepdims=True)
    bound[...] = jnp.broadcast_to(jnp.max(reach, axis=1, keepdims=True), bound.shape)
    sums[0:1, :] = recon_sum
    sums[1:2, :] = jnp.sum(spectral * jnp.log(rebuilt), axis=0, keepdims=True)
    products(1, nt, place, stacked, ratio, away)
    for target in away:
        target[target.shape[0] - 8 :, :] = bound[...]


def products(side, nt, place, stacked, ratio, targets):
    height = stacked.shape[0] // nt
    lap = place[0, 1]
    hop = 1 + ((lap ^ side) & 1)
    order = (3, hop, 3 ^ hop, 0) if nt == 8 else (*range(1, len(targets)), 0)
    for step, target in zip(order, targets):
        at = pl.multiple_of((lap ^ (2 * step + side)) * height, height)
        target[0:height, :] = jnp.dot(
            stacked[pl.ds(at, height), :], ratio[...], preferred_element_type=f32
        )


def kept_kernel(nt, place, stacked, ratio, *targets):
    products(0, nt, place, stacked, ratio, targets)


def message_kernel(bound, kept, crossed, *refs):
    parts, message = refs[:-1], refs[-1]
    height = kept.shape[0]
    limit = bound[0:1, :] + crossed[height : height + 1, :]
    value = kept[...] + crossed[0:height, :]
    for part in parts:
        carried = part[height : height + 1, :]
        limit = limit + carried * 32768.0
        value = value + part[0:height, :] * carried
    unit = jnp.maximum(limit * (1.02 / 32768.0), 2.0**-14).astype(bf16).astype(f32)
    message[0:height, :] = value * (1.0 / unit)
    message[height:, :] = jnp.broadcast_to(unit, (16, kept.shape[1]))


def total_kernel(kept, crossed, *refs):
    parts, total = refs[:-1], refs[-1]
    height = kept.shape[0]
    value = kept[...] + crossed[0:height, :]
    for part in parts:
        value = value + part[0:height, :] * part[height : height + 1, :]
    total[...] = value


def exchanged(value, axis, step):
    size = lax.axis_size(axis)
    return lax.ppermute(value, axis, [(index, index ^ step) for index in range(size)])


def on_device(
    spectrum,
    decay_rate,
    init_state,
    clip_ids,
    encoder,
    gauss_noise,
    uniform_noise,
    boost_count,
    templates,
):
    nt, nf = lax.axis_size("tm"), lax.axis_size("freq")
    bins, frames = spectrum.shape
    topics = encoder.shape[0]
    columns = templates.shape[1]
    piece = frames // nf
    rows = piece + TAIL
    width = -(-rows // LANES) * LANES
    far_first = range(nf - 1, 0, -1)
    place = jnp.stack([lax.axis_index("freq"), lax.axis_index("tm")]).astype(jnp.int32)[None]
    decay = decay_rate[None]
    state_rows = -(-(nf + 1) // 8) * 8
    height = 1 + frames // bins

    *messages, own, flipped, frame_sums = call(
        functools.partial(pieces_kernel, nf),
        "pieces",
        [((rows + topics // 2, bins), bf16)] * (nf - 1)
        + [((rows, bins), bf16), ((frames, bins), bf16), ((frames // bins, bins), f32)],
        [((frames, bins), f32)],
        place,
        jnp.concatenate([spectrum, encoder], axis=1),
        scalars=1,
    )
    small = jnp.pad(decay_rate, (0, frames)) + jnp.pad(clip_ids, (bins, 0)).astype(f32)
    gains, states, tm_message = call(
        functools.partial(summary_kernel, nf),
        "summary",
        [((rows, LANES), f32), ((state_rows, bins), f32), ((height, bins), f32)],
        [((frames, LANES), f32)],
        place,
        flipped,
        small[None],
        scalars=1,
    )
    messages = [exchanged(messages[-step], "freq", step) for step in far_first]
    pair = jnp.concatenate([tm_message, exchanged(tm_message, "tm", 1)], axis=0)
    pairs = [pair] + [exchanged(pair, "tm", step) for step in range(2, nt, 2)]
    stat_rows = columns // bins + frames // bins
    (stats,) = call(
        totals_kernel, "totals", [((stat_rows, bins), f32)], [], templates, frame_sums
    )
    *arrivals, own_state, clips_wide = call(
        functools.partial(entry_kernel, nt, nf),
        "entry",
        [((3 + stat_rows, bins), f32)] * (nf - 1)
        + [((3, bins), f32), ((1, LANES + frames), f32)],
        [((nt, height, bins), f32), ((nt, 1, bins), f32)],
        place,
        decay,
        init_state[None],
        states,
        stats,
        messages[0],
        *pairs,
        scalars=1,
    )
    arrivals = [exchanged(arrivals[-step], "freq", step) for step in far_first]
    noises = call(
        functools.partial(noise_kernel, nf),
        "noise",
        [((topics, width), f32)] * 4,
        [],
        place,
        gauss_noise,
        uniform_noise,
        boost_count[None],
        scalars=1,
    )
    (halves,) = call(
        functools.partial(halves_kernel, rows),
        "halves",
        [(((nf - 1) * topics // 2, bins), bf16)],
        [],
        noises[0],
        *arrivals,
        *messages,
    )
    halves = exchanged(halves, "tm", 1)
    (normed,) = call(
        functools.partial(normed_kernel, nf),
        "normed",
        [((nf, width, bins), bf16)],
        [((nf * bins // LANES, rows, LANES), f32)] * 2,
        own,
        own_state,
        gains,
        *messages,
        *arrivals,
    )
    packed, tail = call(
        functools.partial(sampler_kernel, nf, piece),
        "sampler",
        [((topics * piece // LANES, LANES), bf16), ((topics, LANES), bf16)],
        [],
        place,
        normed,
        encoder,
        halves,
        *noises,
        *messages,
        scalars=1,
    )
    shares = [exchanged(packed, "freq", step) for step in far_first]
    rim = lax.ppermute(tail, "tm", [(index, index + 1) for index in range(nt - 1)])
    height = columns // nt
    stacked, ratio, sums, bound, *away = call(
        functools.partial(rebuild_kernel, nt, nf),
        "rebuild",
        [((columns, frames), bf16), ((frames, bins), bf16), ((8, frames), f32), ((8, bins), f32)]
        + [((height + 8, bins), f32)] * (nt // 2),
        [((topics, LANES + frames), f32), ((16, columns), bf16), ((bins + 16, frames), f32)],
        place,
        packed,
        rim,
        clips_wide,
        templates,
        spectrum,
        stats,
        *shares,
        *arrivals,
        scalars=1,
    )
    steps = [1 << power for power in range(nf.bit_length() - 1)]
    log_sum = sums[1:2] + exchanged(sums[1:2], "freq", steps[0])
    kept = call(
        functools.partial(kept_kernel, nt),
        "kept",
        [((height, bins), f32)] * (nt // 2),
        [],
        place,
        stacked,
        ratio,
        scalars=1,
    )
    crossed = [exchanged(block, "tm", 1) for block in away]

    def sent(index, pairs, *extra):
        (message,) = call(
            message_kernel,
            "message",
            [((height + 16, bins), f32)],
            [],
            bound,
            kept[index],
            crossed[index],
            *extra,
        )
        return lax.ppermute(message.astype(jnp.float16), "tm", pairs).astype(f32)

    if nt == 8:
        first = [(lap, lap ^ (2 << (lap & 1))) for lap in range(nt)]
        second = [(lap, lap ^ (4 >> (lap & 1))) for lap in range(nt)]
        carried = sent(0, first)
        carried, log_sum = lax.optimization_barrier((carried, log_sum))
        parts = [sent(1, first), sent(2, second, carried)]
    else:
        parts = [
            sent(step - 1, [(lap, lap ^ (2 * step)) for lap in range(nt)])
            for step in range(1, nt // 2)
        ]
    (result,) = call(
        total_kernel, "total", [((height, bins), f32)], [], kept[-1], crossed[-1], *parts
    )
    for step in steps[1:]:
        log_sum = log_sum + exchanged(log_sum, "freq", step)
    frame_loss = jnp.log(sums[0]) - log_sum[0] / sums[2]
    return (frame_loss, result)


def solution(mesh):
    placed = (
        P("freq", "tm"),
        P("freq"),
        P("freq"),
        P("tm"),
        P(None, "freq"),
        P(None, "tm"),
        P(None, None, "tm"),
        P(),
        P("freq", None),
    )
    return jax.shard_map(
        on_device, mesh=mesh, in_specs=placed, out_specs=(P("tm"), P("tm", "freq")), check_vma=False
    )
```

```python
import functools

import jax
import jax.numpy as jnp
from jax import lax
from jax.experimental import pallas as pl
from jax.experimental.pallas import tpu as pltpu
from jax.sharding import PartitionSpec as P

F = 1024
K = 256
L = 16
TOP_CLIP = 5
TAIL = 16
LANES = 128
VMEM = pl.BlockSpec(memory_space=pltpu.VMEM)
SMEM = pl.BlockSpec(memory_space=pltpu.SMEM)
f32 = jnp.float32
bf16 = jnp.bfloat16


def call(kernel, name, outs, scratch, *args, scalars=0, limit=12 << 20):
    return pl.pallas_call(
        kernel,
        name=name,
        out_shape=[jax.ShapeDtypeStruct(shape, dtype) for shape, dtype in outs],
        in_specs=[SMEM] * scalars + [VMEM] * (len(args) - scalars),
        out_specs=[VMEM] * len(outs),
        scratch_shapes=[pltpu.VMEM(shape, dtype) for shape, dtype in scratch],
        compiler_params=pltpu.CompilerParams(vmem_limit_bytes=limit),
        cost_estimate=pl.CostEstimate(flops=0, bytes_accessed=0, transcendentals=0),
    )(*args)


def log_keep(decay):
    gap = 1.0 - (1.0 - decay)
    series = gap * (1.0 / 7.0)
    for order in range(6, 0, -1):
        series = gap * (1.0 / order + series)
    return -series


def column(row, lanes=LANES):
    return jnp.transpose(jnp.broadcast_to(row, (lanes, row.shape[1])))


def wide(col, lanes):
    return jnp.concatenate([col] * (lanes // col.shape[1]), axis=1)


def steps_down(size):
    return (size - 1 - lax.broadcasted_iota(jnp.int32, (size, 1), 0)).astype(f32)


def pieces_kernel(nf, place, both, *refs):
    messages, (own, flipped, frame_sums, frames_first) = refs[: nf - 1], refs[nf - 1 :]
    frames, bins = flipped.shape
    spectrum, encoder = both.at[:, 0:frames], both.at[:, frames:]
    piece = frames // nf
    half = encoder.shape[0] // 2
    here, core = place[0, 0], place[0, 1] & 1
    spectral = spectrum[...].astype(f32)
    turned = jnp.transpose(spectral)
    frames_first[...] = turned
    flipped[...] = turned.astype(bf16)
    for step in range(nf):
        target = own if step == 0 else messages[-step]
        start = pl.multiple_of((here ^ step) * piece, piece)
        target[0:piece, :] = frames_first[pl.ds(start, piece), :].astype(bf16)
        target[piece : piece + TAIL, :] = turned[frames - TAIL :].astype(bf16)
        if step:
            low = pl.multiple_of(core * half, half)
            target[piece + TAIL :, :] = encoder[pl.ds(low, half), :]
    total = jnp.sum(spectral, axis=0, keepdims=True)
    for row in range(frames // bins):
        frame_sums[row : row + 1, :] = total[:, row * bins : (row + 1) * bins]


def summary_kernel(nf, place, flipped, small, gains, states, tm_message, all_gains):
    frames, bins = flipped.shape
    piece = frames // nf
    here = place[0, 0]
    clip_row = small[:, bins:]
    clip_col = column(clip_row)
    first = clip_row[:, :1]
    gain = jnp.ones_like(clip_col)
    for value in range(1, TOP_CLIP + 1):
        seen = jnp.max(jnp.where(clip_row == value, 1.0, 0.0), axis=1, keepdims=True)
        counts = (seen > 0.0) & (first < value)
        gain = jnp.where(counts & (clip_col >= value), gain * 0.8, gain)
    all_gains[...] = gain
    start = pl.multiple_of(here * piece, piece)
    gains[0:piece, :] = all_gains[pl.ds(start, piece), :]
    gains[piece:, :] = gain[frames - TAIL :]
    rate = small[:, 0:bins]
    keep = log_keep(rate)
    scaled = flipped[...].astype(f32) * wide(1.0 / gain, bins) * rate
    weights = jnp.exp(steps_down(piece) * keep)
    state = jnp.zeros((1, bins), f32)
    states[...] = jnp.zeros_like(states)
    for index in range(nf):
        states[index : index + 1, :] = state
        rows = scaled[index * piece : (index + 1) * piece]
        if index < nf - 1:
            state = jnp.exp(piece * keep) * state + jnp.sum(rows * weights, axis=0, keepdims=True)
    body = piece - TAIL
    state = jnp.exp(body * keep) * state + jnp.sum(
        rows[:body] * weights[TAIL:], axis=0, keepdims=True
    )
    states[nf : nf + 1, :] = state
    state = jnp.exp(TAIL * keep) * state + jnp.sum(
        rows[body:] * weights[body:], axis=0, keepdims=True
    )
    tm_message[0:1, :] = state
    for row in range(frames // bins):
        tm_message[row + 1 : row + 2, :] = clip_row[:, row * bins : (row + 1) * bins]


def halves_kernel(rows, _, *refs):
    messages = refs[len(refs) // 2 : -1]
    half = messages[0].shape[0] - rows
    for index, message in enumerate(messages):
        refs[-1][index * half : (index + 1) * half, :] = message[rows:, :]


def totals_kernel(templates, frame_sums, stats):
    bins, columns = templates.shape
    for row in range(columns // bins):
        part = templates[:, row * bins : (row + 1) * bins].astype(f32)
        stats[row : row + 1, :] = jnp.sum(part, axis=0, keepdims=True)
    stats[columns // bins : columns // bins + frame_sums.shape[0], :] = frame_sums[...]


def entry_kernel(nt, nf, place, decay, init, states, stats, *refs):
    refs = refs[1:]
    pairs, messages, (own, clips_wide), (blocks, gains) = (
        refs[: nt // 2],
        refs[nt // 2 : nt // 2 + nf - 1],
        refs[nt // 2 + nf - 1 : nt // 2 + nf + 1],
        refs[nt // 2 + nf + 1 :],
    )
    bins = decay.shape[1]
    height = blocks.shape[1]
    frames = (height - 1) * bins
    piece = frames // nf
    here, lap = place[0, 0], place[0, 1]
    for index, pair in enumerate(pairs):
        blocks[2 * index] = pair[0:height]
        blocks[2 * index + 1] = pair[height:]
    ids = blocks[:, 1:, :]
    kinds = jnp.zeros((nt, 1, 1), f32)
    for value in range(TOP_CLIP + 1):
        kinds += jnp.max(jnp.where(ids == value, 1.0, 0.0), axis=(1, 2), keepdims=True)
    gain = jnp.ones_like(kinds)
    for value in range(2, TOP_CLIP + 2):
        gain = jnp.where(kinds >= value, gain * 0.8, gain)
    gains[...] = jnp.broadcast_to(gain, gains.shape)
    keep = log_keep(decay[...])
    through = jnp.exp(frames * keep)
    state = init[...]
    for block in range(nt - 1):
        at, after = block ^ lap, (block + 1) ^ lap
        last = blocks[at, height - 1 : height, bins - 1 : bins]
        first = blocks[after, 1:2, 0:1]
        joint = jnp.where(first != last, 0.8, 1.0)
        passed = joint * (gains[at] * (through * state + blocks[at, 0:1, :]))
        state = jnp.where(block < lap, passed, state)
    tail = jnp.exp((frames - TAIL) * keep) * state + states[nf : nf + 1, :]
    for step in range(nf):
        target = own if step == 0 else messages[-step]
        other = here ^ step
        power = jnp.exp((other * piece).astype(f32) * keep)
        target[0:1, :] = power * state + states[pl.ds(other, 1), :]
        target[1:2, :] = tail
        target[2:3, :] = decay[...]
        if step:
            target[3:, :] = stats[...]
    previous = blocks[jnp.maximum(lap - 1, 0) ^ lap, height - 1 : height, bins - LANES : bins]
    clips_wide[:, 0:LANES] = jnp.where(lap > 0, previous, -1.0)
    for row in range(frames // bins):
        low = LANES + row * bins
        clips_wide[:, low : low + bins] = blocks[0, row + 1 : row + 2, :]


def noise_kernel(nf, place, gauss, uniform, boost, normal, first, second, boosts):
    topics, frames = gauss.shape
    piece = frames // nf
    here = place[0, 0]
    width = normal.shape[1]
    counts = wide(column(boost[...].astype(f32)), width)
    boosts[...] = counts
    normal[...] = jnp.zeros_like(normal)
    first[...] = jnp.ones_like(first)
    second[...] = jnp.ones_like(second)
    pairs = ((gauss, normal), (uniform.at[0], first), (uniform.at[1], second))
    for index in range(nf):

        @pl.when(here == index)
        def _():
            for source, target in pairs:
                target[:, 0:piece] = source[:, index * piece : (index + 1) * piece]

    for source, target in pairs:
        target[:, piece : piece + TAIL] = source[:, frames - TAIL :]
    first[...] = jnp.log(first[...])
    second[...] = jnp.where(counts >= 2.0, jnp.log(second[...]), 0.0)


def normed_kernel(nf, own, own_state, gains, *refs):
    messages, arrivals, (normed, inputs, running) = (
        refs[: nf - 1],
        refs[nf - 1 : 2 * nf - 2],
        refs[2 * nf - 2 :],
    )
    rows, bins = own.shape
    piece = rows - TAIL
    segment = piece // 8
    gain = gains[...]
    inverse = 1.0 / gain
    powers = (1 + lax.broadcasted_iota(jnp.int32, (segment, 1), 0)).astype(f32)
    normed[:, rows:, :] = jnp.zeros_like(normed[:, rows:, :])
    for step in range(nf):
        state = own_state if step == 0 else arrivals[-step]
        block = own if step == 0 else messages[-step]
        for part in range(bins // LANES):
            at = step * (bins // LANES) + part
            lanes = slice(part * LANES, (part + 1) * LANES)
            spectral = block[0:rows, lanes].astype(f32)
            rate = state[2:3, lanes]
            keep = log_keep(rate)
            fade = 1.0 - rate
            inputs[at] = spectral * inverse * rate
            total = jnp.zeros((8, LANES), f32)
            for row in range(segment):
                total = fade * total + inputs[at, pl.ds(row, 8, stride=segment), :]
                running[at, pl.ds(row, 8, stride=segment), :] = total
            carry = state[0:1, lanes]
            through = jnp.exp(segment * keep)
            fading = jnp.exp(powers * keep)
            for index in range(8):
                low = index * segment
                running[at, low : low + segment, :] += fading * carry
                carry = through * carry + total[index : index + 1, :]
            carry = state[1:2, lanes]
            for row in range(piece, rows):
                carry = fade * carry + inputs[at, row : row + 1, :]
                running[at, row : row + 1, :] = carry
            smooth = running[at] * gain
            normed[step, 0:rows, lanes] = (spectral * lax.rsqrt(smooth + 0.1)).astype(bf16)


def sampler_kernel(nf, piece, place, normed, encoder, halves, normal, first, second, boosts, *refs):
    messages, (packed, tail) = refs[: nf - 1], refs[nf - 1 :]
    core = place[0, 1] & 1
    topics, width = normal.shape
    half = topics // 2
    rows = piece + TAIL
    logits = jnp.zeros((topics, width), f32)
    for step in range(nf):
        if step == 0:
            weights = encoder[...]
        else:
            mine = messages[-step][rows:, :]
            other = halves[(nf - 1 - step) * half : (nf - step) * half, :]
            lower = jnp.where(core == 0, mine, other)
            upper = jnp.where(core == 0, other, mine)
            weights = jnp.concatenate([lower, upper], axis=0)
        logits += lax.dot_general(
            weights, normed[step], (((1,), (1,)), ((), ())), preferred_element_type=f32
        )
    concentration = jnp.maximum(logits, 0.0) + jnp.log1p(jnp.exp(-jnp.abs(logits))) + 0.5
    offset = concentration + boosts[...] - 1.0 / 3.0
    linear = 1.0 + lax.rsqrt(9.0 * offset) * normal[...]
    draw = offset * linear * linear * linear
    draw = draw * jnp.exp(first[...] / concentration + second[...] / (concentration + 1.0))
    proportions = draw / jnp.sum(draw, axis=0, keepdims=True)
    full, rest = piece // LANES, piece % LANES
    for index in range(full):
        tile = proportions[:, index * LANES : (index + 1) * LANES]
        packed[index * topics : (index + 1) * topics, :] = tile.astype(bf16)
    tile = proportions[:, full * LANES : (full + 1) * LANES]
    if rest:
        lane = lax.broadcasted_iota(jnp.int32, (half, LANES), 1)
        joined = jnp.where(lane < rest, tile[:half], pltpu.roll(tile[half:], rest, 1))
        packed[full * topics :, :] = joined.astype(bf16)
    tail[...] = pltpu.roll(tile, LANES - TAIL - rest, 1).astype(bf16)


def rebuild_kernel(nt, nf, place, own, rim, clips, templates, spectrum, stats, *refs):
    messages, arrivals, (stacked, ratio, sums, bound, *away, extended, heads, recon) = (
        refs[: nf - 1],
        refs[nf - 1 : 2 * nf - 2],
        refs[2 * nf - 2 :],
    )
    bins, frames = spectrum.shape
    here = place[0, 0]
    piece = frames // nf
    topics = extended.shape[0]
    full, rest = piece // LANES, piece % LANES
    extended[:, 0:LANES] = rim[...].astype(f32)
    for step in range(nf):
        source = own if step == 0 else messages[-step]
        for index in range(nf):

            @pl.when((here ^ step) == index)
            def _():
                low = LANES + index * piece
                for part in range(full):
                    values = source[part * topics : (part + 1) * topics, :].astype(f32)
                    extended[:, low + part * LANES : low + (part + 1) * LANES] = values
                if rest:
                    values = source[full * topics :, :].astype(f32)
                    low += full * LANES
                    half = topics // 2
                    extended[0:half, low : low + rest] = values[:, 0:rest]
                    extended[half:, low : low + rest] = values[:, rest:]

    total = stats[...]
    for arrival in arrivals:
        total = total + arrival[3:, :]
    columns = templates.shape[1]
    wide_rows = columns // bins
    heads[...] = jnp.zeros_like(heads)
    for row in range(wide_rows):
        value = total[row : row + 1, :]
        for index in range(3):
            rounded = value.astype(bf16)
            heads[index : index + 1, row * bins : (row + 1) * bins] = rounded
            value = value - rounded.astype(f32)
    for row in range(frames // bins):
        at = wide_rows + row
        sums[2:3, row * bins : (row + 1) * bins] = total[at : at + 1, :]
    ids = jnp.broadcast_to(clips[...], (L, LANES + frames))
    shifted = pltpu.roll(ids, 0, 1, stride=1, stride_axis=0)
    valid = jnp.where(shifted == ids, 1.0, 0.0)[:, LANES:].astype(bf16)
    group = 32
    for low in range(0, topics, group):
        for topic in range(low, low + group):
            row = jnp.broadcast_to(extended[topic : topic + 1, :], (L, LANES + frames))
            lagged = pltpu.roll(row, 0, 1, stride=1, stride_axis=0)[:, LANES:]
            stacked[topic * L : (topic + 1) * L, :] = lagged.astype(bf16) * valid
        part = slice(low * L, (low + group) * L)
        left = jnp.concatenate([templates[:, part], heads[:, part]], axis=0)
        product = jnp.dot(left, stacked[part, :], preferred_element_type=f32)
        if low == 0:
            recon[...] = product
        else:
            recon[...] += product
    rebuilt = recon[0:bins, :]
    recon_sum = recon[bins : bins + 1] + recon[bins + 1 : bins + 2] + recon[bins + 2 : bins + 3]
    spectral = spectrum[...].astype(f32)
    scale = F * K / (frames * nt)
    rounded = (scale * (1.0 / recon_sum - spectral / (sums[2:3, :] * rebuilt))).astype(bf16)
    turned = jnp.transpose(rounded.astype(f32))
    ratio[...] = turned.astype(bf16)
    reach = jnp.sum(jnp.abs(turned), axis=0, keepdims=True)
    bound[...] = jnp.broadcast_to(jnp.max(reach, axis=1, keepdims=True), bound.shape)
    sums[0:1, :] = recon_sum
    sums[1:2, :] = jnp.sum(spectral * jnp.log(rebuilt), axis=0, keepdims=True)
    products(1, nt, place, stacked, ratio, away)
    for target in away:
        target[target.shape[0] - 8 :, :] = bound[...]


def products(side, nt, place, stacked, ratio, targets):
    height = stacked.shape[0] // nt
    lap = place[0, 1]
    hop = 1 + ((lap ^ side) & 1)
    order = (3, hop, 3 ^ hop, 0) if nt == 8 else (*range(1, len(targets)), 0)
    for step, target in zip(order, targets):
        at = pl.multiple_of((lap ^ (2 * step + side)) * height, height)
        target[0:height, :] = jnp.dot(
            stacked[pl.ds(at, height), :], ratio[...], preferred_element_type=f32
        )


def kept_kernel(nt, place, stacked, ratio, *targets):
    products(0, nt, place, stacked, ratio, targets)


def message_kernel(bound, kept, crossed, *refs):
    parts, message = refs[:-1], refs[-1]
    height = kept.shape[0]
    limit = bound[0:1, :] + crossed[height : height + 1, :]
    value = kept[...] + crossed[0:height, :]
    for part in parts:
        carried = part[height : height + 1, :]
        limit = limit + carried * 32768.0
        value = value + part[0:height, :] * carried
    unit = jnp.maximum(limit * (1.02 / 32768.0), 2.0**-14).astype(bf16).astype(f32)
    message[0:height, :] = value * (1.0 / unit)
    message[height:, :] = jnp.broadcast_to(unit, (16, kept.shape[1]))


def total_kernel(kept, crossed, *refs):
    parts, total = refs[:-1], refs[-1]
    height = kept.shape[0]
    value = kept[...] + crossed[0:height, :]
    for part in parts:
        value = value + part[0:height, :] * part[height : height + 1, :]
    total[...] = value


def exchanged(value, axis, step):
    size = lax.axis_size(axis)
    return lax.ppermute(value, axis, [(index, index ^ step) for index in range(size)])


def on_device(
    spectrum,
    decay_rate,
    init_state,
    clip_ids,
    encoder,
    gauss_noise,
    uniform_noise,
    boost_count,
    templates,
):
    nt, nf = lax.axis_size("tm"), lax.axis_size("freq")
    bins, frames = spectrum.shape
    topics = encoder.shape[0]
    columns = templates.shape[1]
    piece = frames // nf
    rows = piece + TAIL
    width = -(-rows // LANES) * LANES
    far_first = range(nf - 1, 0, -1)
    place = jnp.stack([lax.axis_index("freq"), lax.axis_index("tm")]).astype(jnp.int32)[None]
    decay = decay_rate[None]
    state_rows = -(-(nf + 1) // 8) * 8
    height = 1 + frames // bins

    *messages, own, flipped, frame_sums = call(
        functools.partial(pieces_kernel, nf),
        "pieces",
        [((rows + topics // 2, bins), bf16)] * (nf - 1)
        + [((rows, bins), bf16), ((frames, bins), bf16), ((frames // bins, bins), f32)],
        [((frames, bins), f32)],
        place,
        jnp.concatenate([spectrum, encoder], axis=1),
        scalars=1,
    )
    small = jnp.pad(decay_rate, (0, frames)) + jnp.pad(clip_ids, (bins, 0)).astype(f32)
    gains, states, tm_message = call(
        functools.partial(summary_kernel, nf),
        "summary",
        [((rows, LANES), f32), ((state_rows, bins), f32), ((height, bins), f32)],
        [((frames, LANES), f32)],
        place,
        flipped,
        small[None],
        scalars=1,
    )
    messages = [exchanged(messages[-step], "freq", step) for step in far_first]
    pair = jnp.concatenate([tm_message, exchanged(tm_message, "tm", 1)], axis=0)
    pairs = [pair] + [exchanged(pair, "tm", step) for step in range(2, nt, 2)]
    stat_rows = columns // bins + frames // bins
    (stats,) = call(
        totals_kernel, "totals", [((stat_rows, bins), f32)], [], templates, frame_sums
    )
    *arrivals, own_state, clips_wide = call(
        functools.partial(entry_kernel, nt, nf),
        "entry",
        [((3 + stat_rows, bins), f32)] * (nf - 1)
        + [((3, bins), f32), ((1, LANES + frames), f32)],
        [((nt, height, bins), f32), ((nt, 1, bins), f32)],
        place,
        decay,
        init_state[None],
        states,
        stats,
        messages[0],
        *pairs,
        scalars=1,
    )
    arrivals = [exchanged(arrivals[-step], "freq", step) for step in far_first]
    noises = call(
        functools.partial(noise_kernel, nf),
        "noise",
        [((topics, width), f32)] * 4,
        [],
        place,
        gauss_noise,
        uniform_noise,
        boost_count[None],
        scalars=1,
    )
    (halves,) = call(
        functools.partial(halves_kernel, rows),
        "halves",
        [(((nf - 1) * topics // 2, bins), bf16)],
        [],
        noises[0],
        *arrivals,
        *messages,
    )
    halves = exchanged(halves, "tm", 1)
    (normed,) = call(
        functools.partial(normed_kernel, nf),
        "normed",
        [((nf, width, bins), bf16)],
        [((nf * bins // LANES, rows, LANES), f32)] * 2,
        own,
        own_state,
        gains,
        *messages,
        *arrivals,
    )
    packed, tail = call(
        functools.partial(sampler_kernel, nf, piece),
        "sampler",
        [((topics * piece // LANES, LANES), bf16), ((topics, LANES), bf16)],
        [],
        place,
        normed,
        encoder,
        halves,
        *noises,
        *messages,
        scalars=1,
    )
    shares = [exchanged(packed, "freq", step) for step in far_first]
    rim = lax.ppermute(tail, "tm", [(index, index + 1) for index in range(nt - 1)])
    height = columns // nt
    stacked, ratio, sums, bound, *away = call(
        functools.partial(rebuild_kernel, nt, nf),
        "rebuild",
        [((columns, frames), bf16), ((frames, bins), bf16), ((8, frames), f32), ((8, bins), f32)]
        + [((height + 8, bins), f32)] * (nt // 2),
        [((topics, LANES + frames), f32), ((16, columns), bf16), ((bins + 16, frames), f32)],
        place,
        packed,
        rim,
        clips_wide,
        templates,
        spectrum,
        stats,
        *shares,
        *arrivals,
        scalars=1,
    )
    steps = [1 << power for power in range(nf.bit_length() - 1)]
    kept = call(
        functools.partial(kept_kernel, nt),
        "kept",
        [((height, bins), f32)] * (nt // 2),
        [],
        place,
        stacked,
        ratio,
        scalars=1,
    )
    crossed = [exchanged(block, "tm", 1) for block in away]

    def message_of(index, *extra):
        (message,) = call(
            message_kernel,
            "message",
            [((height + 16, bins), f32)],
            [],
            bound,
            kept[index],
            crossed[index],
            *extra,
        )
        return message.astype(jnp.float16)

    def sent(message, pairs):
        return lax.ppermute(message, "tm", pairs).astype(f32)

    log_sum = sums[1:2]
    if nt == 8:
        first = [(lap, lap ^ (2 << (lap & 1))) for lap in range(nt)]
        second = [(lap, lap ^ (4 >> (lap & 1))) for lap in range(nt)]
        carried = sent(message_of(0), first)
        direct, log_sum = lax.optimization_barrier((message_of(1), log_sum))
        parts = [sent(direct, first)]
        log_sum = log_sum + exchanged(log_sum, "freq", steps[0])
        carried, log_sum = lax.optimization_barrier((carried, log_sum))
        parts.append(sent(message_of(2, carried), second))
    else:
        log_sum = log_sum + exchanged(log_sum, "freq", steps[0])
        parts = [
            sent(message_of(step - 1), [(lap, lap ^ (2 * step)) for lap in range(nt)])
            for step in range(1, nt // 2)
        ]
    (result,) = call(
        total_kernel, "total", [((height, bins), f32)], [], kept[-1], crossed[-1], *parts
    )
    for step in steps[1:]:
        log_sum = log_sum + exchanged(log_sum, "freq", step)
    frame_loss = jnp.log(sums[0]) - log_sum[0] / sums[2]
    return (frame_loss, result)


def solution(mesh):
    placed = (
        P("freq", "tm"),
        P("freq"),
        P("freq"),
        P("tm"),
        P(None, "freq"),
        P(None, "tm"),
        P(None, None, "tm"),
        P(),
        P("freq", None),
    )
    return jax.shard_map(
        on_device, mesh=mesh, in_specs=placed, out_specs=(P("tm"), P("tm", "freq")), check_vma=False
    )
```

```python
import functools

import jax
import jax.numpy as jnp
from jax import lax
from jax.experimental import pallas as pl
from jax.experimental.pallas import tpu as pltpu
from jax.sharding import PartitionSpec as P

F = 1024
K = 256
L = 16
TOP_CLIP = 5
TAIL = 16
LANES = 128
VMEM = pl.BlockSpec(memory_space=pltpu.VMEM)
SMEM = pl.BlockSpec(memory_space=pltpu.SMEM)
f32 = jnp.float32
bf16 = jnp.bfloat16


def call(kernel, name, outs, scratch, *args, scalars=0, limit=12 << 20):
    return pl.pallas_call(
        kernel,
        name=name,
        out_shape=[jax.ShapeDtypeStruct(shape, dtype) for shape, dtype in outs],
        in_specs=[SMEM] * scalars + [VMEM] * (len(args) - scalars),
        out_specs=[VMEM] * len(outs),
        scratch_shapes=[pltpu.VMEM(shape, dtype) for shape, dtype in scratch],
        compiler_params=pltpu.CompilerParams(vmem_limit_bytes=limit),
        cost_estimate=pl.CostEstimate(flops=0, bytes_accessed=0, transcendentals=0),
    )(*args)


def log_keep(decay):
    gap = 1.0 - (1.0 - decay)
    series = gap * (1.0 / 7.0)
    for order in range(6, 0, -1):
        series = gap * (1.0 / order + series)
    return -series


def column(row, lanes=LANES):
    return jnp.transpose(jnp.broadcast_to(row, (lanes, row.shape[1])))


def wide(col, lanes):
    return jnp.concatenate([col] * (lanes // col.shape[1]), axis=1)


def steps_down(size):
    return (size - 1 - lax.broadcasted_iota(jnp.int32, (size, 1), 0)).astype(f32)


def pieces_kernel(nf, place, both, *refs):
    messages, (own, flipped, frame_sums, frames_first) = refs[: nf - 1], refs[nf - 1 :]
    frames, bins = flipped.shape
    spectrum, encoder = both.at[:, 0:frames], both.at[:, frames:]
    piece = frames // nf
    half = encoder.shape[0] // 2
    here, core = place[0, 0], place[0, 1] & 1
    spectral = spectrum[...].astype(f32)
    turned = jnp.transpose(spectral)
    frames_first[...] = turned
    flipped[...] = turned.astype(bf16)
    for step in range(nf):
        target = own if step == 0 else messages[-step]
        start = pl.multiple_of((here ^ step) * piece, piece)
        target[0:piece, :] = frames_first[pl.ds(start, piece), :].astype(bf16)
        target[piece : piece + TAIL, :] = turned[frames - TAIL :].astype(bf16)
        if step:
            low = pl.multiple_of(core * half, half)
            target[piece + TAIL :, :] = encoder[pl.ds(low, half), :]
    total = jnp.sum(spectral, axis=0, keepdims=True)
    for row in range(frames // bins):
        frame_sums[row : row + 1, :] = total[:, row * bins : (row + 1) * bins]


def summary_kernel(nf, place, flipped, small, gains, states, tm_message, all_gains):
    frames, bins = flipped.shape
    piece = frames // nf
    here = place[0, 0]
    clip_row = small[:, bins:]
    clip_col = column(clip_row)
    first = clip_row[:, :1]
    gain = jnp.ones_like(clip_col)
    for value in range(1, TOP_CLIP + 1):
        seen = jnp.max(jnp.where(clip_row == value, 1.0, 0.0), axis=1, keepdims=True)
        counts = (seen > 0.0) & (first < value)
        gain = jnp.where(counts & (clip_col >= value), gain * 0.8, gain)
    all_gains[...] = gain
    start = pl.multiple_of(here * piece, piece)
    gains[0:piece, :] = all_gains[pl.ds(start, piece), :]
    gains[piece:, :] = gain[frames - TAIL :]
    rate = small[:, 0:bins]
    keep = log_keep(rate)
    scaled = flipped[...].astype(f32) * wide(1.0 / gain, bins) * rate
    weights = jnp.exp(steps_down(piece) * keep)
    state = jnp.zeros((1, bins), f32)
    states[...] = jnp.zeros_like(states)
    for index in range(nf):
        states[index : index + 1, :] = state
        rows = scaled[index * piece : (index + 1) * piece]
        if index < nf - 1:
            state = jnp.exp(piece * keep) * state + jnp.sum(rows * weights, axis=0, keepdims=True)
    body = piece - TAIL
    state = jnp.exp(body * keep) * state + jnp.sum(
        rows[:body] * weights[TAIL:], axis=0, keepdims=True
    )
    states[nf : nf + 1, :] = state
    state = jnp.exp(TAIL * keep) * state + jnp.sum(
        rows[body:] * weights[body:], axis=0, keepdims=True
    )
    tm_message[0:1, :] = state
    for row in range(frames // bins):
        tm_message[row + 1 : row + 2, :] = clip_row[:, row * bins : (row + 1) * bins]


def halves_kernel(rows, _, *refs):
    messages = refs[len(refs) // 2 : -1]
    half = messages[0].shape[0] - rows
    for index, message in enumerate(messages):
        refs[-1][index * half : (index + 1) * half, :] = message[rows:, :]


def totals_kernel(templates, frame_sums, stats):
    bins, columns = templates.shape
    for row in range(columns // bins):
        part = templates[:, row * bins : (row + 1) * bins].astype(f32)
        stats[row : row + 1, :] = jnp.sum(part, axis=0, keepdims=True)
    stats[columns // bins : columns // bins + frame_sums.shape[0], :] = frame_sums[...]


def entry_kernel(nt, nf, place, decay, init, states, stats, *refs):
    refs = refs[1:]
    pairs, messages, (own, clips_wide), (blocks, gains) = (
        refs[: nt // 2],
        refs[nt // 2 : nt // 2 + nf - 1],
        refs[nt // 2 + nf - 1 : nt // 2 + nf + 1],
        refs[nt // 2 + nf + 1 :],
    )
    bins = decay.shape[1]
    height = blocks.shape[1]
    frames = (height - 1) * bins
    piece = frames // nf
    here, lap = place[0, 0], place[0, 1]
    for index, pair in enumerate(pairs):
        blocks[2 * index] = pair[0:height]
        blocks[2 * index + 1] = pair[height:]
    ids = blocks[:, 1:, :]
    kinds = jnp.zeros((nt, 1, 1), f32)
    for value in range(TOP_CLIP + 1):
        kinds += jnp.max(jnp.where(ids == value, 1.0, 0.0), axis=(1, 2), keepdims=True)
    gain = jnp.ones_like(kinds)
    for value in range(2, TOP_CLIP + 2):
        gain = jnp.where(kinds >= value, gain * 0.8, gain)
    gains[...] = jnp.broadcast_to(gain, gains.shape)
    keep = log_keep(decay[...])
    through = jnp.exp(frames * keep)
    state = init[...]
    for block in range(nt - 1):
        at, after = block ^ lap, (block + 1) ^ lap
        last = blocks[at, height - 1 : height, bins - 1 : bins]
        first = blocks[after, 1:2, 0:1]
        joint = jnp.where(first != last, 0.8, 1.0)
        passed = joint * (gains[at] * (through * state + blocks[at, 0:1, :]))
        state = jnp.where(block < lap, passed, state)
    tail = jnp.exp((frames - TAIL) * keep) * state + states[nf : nf + 1, :]
    for step in range(nf):
        target = own if step == 0 else messages[-step]
        other = here ^ step
        power = jnp.exp((other * piece).astype(f32) * keep)
        target[0:1, :] = power * state + states[pl.ds(other, 1), :]
        target[1:2, :] = tail
        target[2:3, :] = decay[...]
        if step:
            target[3:, :] = stats[...]
    previous = blocks[jnp.maximum(lap - 1, 0) ^ lap, height - 1 : height, bins - LANES : bins]
    clips_wide[:, 0:LANES] = jnp.where(lap > 0, previous, -1.0)
    for row in range(frames // bins):
        low = LANES + row * bins
        clips_wide[:, low : low + bins] = blocks[0, row + 1 : row + 2, :]


def noise_kernel(nf, place, gauss, uniform, boost, normal, first, second, boosts):
    topics, frames = gauss.shape
    piece = frames // nf
    here = place[0, 0]
    width = normal.shape[1]
    counts = wide(column(boost[...].astype(f32)), width)
    boosts[...] = counts
    normal[...] = jnp.zeros_like(normal)
    first[...] = jnp.ones_like(first)
    second[...] = jnp.ones_like(second)
    pairs = ((gauss, normal), (uniform.at[0], first), (uniform.at[1], second))
    for index in range(nf):

        @pl.when(here == index)
        def _():
            for source, target in pairs:
                target[:, 0:piece] = source[:, index * piece : (index + 1) * piece]

    for source, target in pairs:
        target[:, piece : piece + TAIL] = source[:, frames - TAIL :]
    first[...] = jnp.log(first[...])
    second[...] = jnp.where(counts >= 2.0, jnp.log(second[...]), 0.0)


def normed_kernel(nf, own, own_state, gains, *refs):
    messages, arrivals, (normed, inputs, running) = (
        refs[: nf - 1],
        refs[nf - 1 : 2 * nf - 2],
        refs[2 * nf - 2 :],
    )
    rows, bins = own.shape
    piece = rows - TAIL
    segment = piece // 8
    gain = gains[...]
    inverse = 1.0 / gain
    powers = (1 + lax.broadcasted_iota(jnp.int32, (segment, 1), 0)).astype(f32)
    normed[:, rows:, :] = jnp.zeros_like(normed[:, rows:, :])
    for step in range(nf):
        state = own_state if step == 0 else arrivals[-step]
        block = own if step == 0 else messages[-step]
        for part in range(bins // LANES):
            at = step * (bins // LANES) + part
            lanes = slice(part * LANES, (part + 1) * LANES)
            spectral = block[0:rows, lanes].astype(f32)
            rate = state[2:3, lanes]
            keep = log_keep(rate)
            fade = 1.0 - rate
            inputs[at] = spectral * inverse * rate
            total = jnp.zeros((8, LANES), f32)
            for row in range(segment):
                total = fade * total + inputs[at, pl.ds(row, 8, stride=segment), :]
                running[at, pl.ds(row, 8, stride=segment), :] = total
            carry = state[0:1, lanes]
            through = jnp.exp(segment * keep)
            fading = jnp.exp(powers * keep)
            for index in range(8):
                low = index * segment
                running[at, low : low + segment, :] += fading * carry
                carry = through * carry + total[index : index + 1, :]
            carry = state[1:2, lanes]
            for row in range(piece, rows):
                carry = fade * carry + inputs[at, row : row + 1, :]
                running[at, row : row + 1, :] = carry
            smooth = running[at] * gain
            normed[step, 0:rows, lanes] = (spectral * lax.rsqrt(smooth + 0.1)).astype(bf16)


def sampler_kernel(nf, piece, place, normed, encoder, halves, normal, first, second, boosts, *refs):
    messages, (packed, tail) = refs[: nf - 1], refs[nf - 1 :]
    core = place[0, 1] & 1
    topics, width = normal.shape
    half = topics // 2
    rows = piece + TAIL
    logits = jnp.zeros((topics, width), f32)
    for step in range(nf):
        if step == 0:
            weights = encoder[...]
        else:
            mine = messages[-step][rows:, :]
            other = halves[(nf - 1 - step) * half : (nf - step) * half, :]
            lower = jnp.where(core == 0, mine, other)
            upper = jnp.where(core == 0, other, mine)
            weights = jnp.concatenate([lower, upper], axis=0)
        logits += lax.dot_general(
            weights, normed[step], (((1,), (1,)), ((), ())), preferred_element_type=f32
        )
    concentration = jnp.maximum(logits, 0.0) + jnp.log1p(jnp.exp(-jnp.abs(logits))) + 0.5
    offset = concentration + boosts[...] - 1.0 / 3.0
    linear = 1.0 + lax.rsqrt(9.0 * offset) * normal[...]
    draw = offset * linear * linear * linear
    draw = draw * jnp.exp(first[...] / concentration + second[...] / (concentration + 1.0))
    proportions = draw / jnp.sum(draw, axis=0, keepdims=True)
    full, rest = piece // LANES, piece % LANES
    for index in range(full):
        tile = proportions[:, index * LANES : (index + 1) * LANES]
        packed[index * topics : (index + 1) * topics, :] = tile.astype(bf16)
    tile = proportions[:, full * LANES : (full + 1) * LANES]
    if rest:
        lane = lax.broadcasted_iota(jnp.int32, (half, LANES), 1)
        joined = jnp.where(lane < rest, tile[:half], pltpu.roll(tile[half:], rest, 1))
        packed[full * topics :, :] = joined.astype(bf16)
    tail[...] = pltpu.roll(tile, LANES - TAIL - rest, 1).astype(bf16)


def rebuild_kernel(nt, nf, place, own, rim, clips, templates, spectrum, stats, *refs):
    messages, arrivals, (stacked, ratio, sums, bound, *away, extended, heads, recon) = (
        refs[: nf - 1],
        refs[nf - 1 : 2 * nf - 2],
        refs[2 * nf - 2 :],
    )
    bins, frames = spectrum.shape
    here = place[0, 0]
    piece = frames // nf
    topics = extended.shape[0]
    full, rest = piece // LANES, piece % LANES
    extended[:, 0:LANES] = rim[...].astype(f32)
    for step in range(nf):
        source = own if step == 0 else messages[-step]
        for index in range(nf):

            @pl.when((here ^ step) == index)
            def _():
                low = LANES + index * piece
                for part in range(full):
                    values = source[part * topics : (part + 1) * topics, :].astype(f32)
                    extended[:, low + part * LANES : low + (part + 1) * LANES] = values
                if rest:
                    values = source[full * topics :, :].astype(f32)
                    low += full * LANES
                    half = topics // 2
                    extended[0:half, low : low + rest] = values[:, 0:rest]
                    extended[half:, low : low + rest] = values[:, rest:]

    total = stats[...]
    for arrival in arrivals:
        total = total + arrival[3:, :]
    columns = templates.shape[1]
    wide_rows = columns // bins
    heads[...] = jnp.zeros_like(heads)
    for row in range(wide_rows):
        value = total[row : row + 1, :]
        for index in range(3):
            rounded = value.astype(bf16)
            heads[index : index + 1, row * bins : (row + 1) * bins] = rounded
            value = value - rounded.astype(f32)
    for row in range(frames // bins):
        at = wide_rows + row
        sums[2:3, row * bins : (row + 1) * bins] = total[at : at + 1, :]
    ids = jnp.broadcast_to(clips[...], (L, LANES + frames))
    shifted = pltpu.roll(ids, 0, 1, stride=1, stride_axis=0)
    valid = jnp.where(shifted == ids, 1.0, 0.0)[:, LANES:].astype(bf16)
    group = 32
    for low in range(0, topics, group):
        for topic in range(low, low + group):
            row = jnp.broadcast_to(extended[topic : topic + 1, :], (L, LANES + frames))
            lagged = pltpu.roll(row, 0, 1, stride=1, stride_axis=0)[:, LANES:]
            stacked[topic * L : (topic + 1) * L, :] = lagged.astype(bf16) * valid
        part = slice(low * L, (low + group) * L)
        left = jnp.concatenate([templates[:, part], heads[:, part]], axis=0)
        product = jnp.dot(left, stacked[part, :], preferred_element_type=f32)
        if low == 0:
            recon[...] = product
        else:
            recon[...] += product
    rebuilt = recon[0:bins, :]
    recon_sum = recon[bins : bins + 1] + recon[bins + 1 : bins + 2] + recon[bins + 2 : bins + 3]
    spectral = spectrum[...].astype(f32)
    scale = F * K / (frames * nt)
    rounded = (scale * (1.0 / recon_sum - spectral / (sums[2:3, :] * rebuilt))).astype(bf16)
    turned = jnp.transpose(rounded.astype(f32))
    ratio[...] = turned.astype(bf16)
    reach = jnp.sum(jnp.abs(turned), axis=0, keepdims=True)
    bound[...] = jnp.broadcast_to(jnp.max(reach, axis=1, keepdims=True), bound.shape)
    sums[0:1, :] = recon_sum
    sums[1:2, :] = jnp.sum(spectral * jnp.log(rebuilt), axis=0, keepdims=True)
    products(1, nt, place, stacked, ratio, away)
    for target in away:
        target[target.shape[0] - 8 :, :] = bound[...]


def products(side, nt, place, stacked, ratio, targets):
    height = stacked.shape[0] // nt
    lap = place[0, 1]
    hop = 1 + ((lap ^ side) & 1)
    order = (3, hop, 3 ^ hop, 0) if nt == 8 else (*range(1, len(targets)), 0)
    for step, target in zip(order, targets):
        at = pl.multiple_of((lap ^ (2 * step + side)) * height, height)
        target[0:height, :] = jnp.dot(
            stacked[pl.ds(at, height), :], ratio[...], preferred_element_type=f32
        )


def kept_kernel(nt, place, stacked, ratio, *targets):
    products(0, nt, place, stacked, ratio, targets)


def message_kernel(bound, kept, crossed, *refs):
    parts, message = refs[:-1], refs[-1]
    height = kept.shape[0]
    limit = bound[0:1, :] + crossed[height : height + 1, :]
    value = kept[...] + crossed[0:height, :]
    for part in parts:
        carried = part[height : height + 1, :]
        limit = limit + carried * 32768.0
        value = value + part[0:height, :] * carried
    unit = jnp.maximum(limit * (1.02 / 32768.0), 2.0**-14).astype(bf16).astype(f32)
    message[0:height, :] = value * (1.0 / unit)
    message[height:, :] = jnp.broadcast_to(unit, (16, kept.shape[1]))


def total_kernel(kept, crossed, *refs):
    parts, total = refs[:-1], refs[-1]
    height = kept.shape[0]
    value = kept[...] + crossed[0:height, :]
    for part in parts:
        value = value + part[0:height, :] * part[height : height + 1, :]
    total[...] = value


def exchanged(value, axis, step):
    size = lax.axis_size(axis)
    return lax.ppermute(value, axis, [(index, index ^ step) for index in range(size)])


def on_device(
    spectrum,
    decay_rate,
    init_state,
    clip_ids,
    encoder,
    gauss_noise,
    uniform_noise,
    boost_count,
    templates,
):
    nt, nf = lax.axis_size("tm"), lax.axis_size("freq")
    bins, frames = spectrum.shape
    topics = encoder.shape[0]
    columns = templates.shape[1]
    piece = frames // nf
    rows = piece + TAIL
    width = -(-rows // LANES) * LANES
    far_first = range(nf - 1, 0, -1)
    place = jnp.stack([lax.axis_index("freq"), lax.axis_index("tm")]).astype(jnp.int32)[None]
    decay = decay_rate[None]
    state_rows = -(-(nf + 1) // 8) * 8
    height = 1 + frames // bins

    *messages, own, flipped, frame_sums = call(
        functools.partial(pieces_kernel, nf),
        "pieces",
        [((rows + topics // 2, bins), bf16)] * (nf - 1)
        + [((rows, bins), bf16), ((frames, bins), bf16), ((frames // bins, bins), f32)],
        [((frames, bins), f32)],
        place,
        jnp.concatenate([spectrum, encoder], axis=1),
        scalars=1,
    )
    small = jnp.pad(decay_rate, (0, frames)) + jnp.pad(clip_ids, (bins, 0)).astype(f32)
    gains, states, tm_message = call(
        functools.partial(summary_kernel, nf),
        "summary",
        [((rows, LANES), f32), ((state_rows, bins), f32), ((height, bins), f32)],
        [((frames, LANES), f32)],
        place,
        flipped,
        small[None],
        scalars=1,
    )
    *messages, nearest = [
        exchanged(messages[-step], "freq", step) if step > 1 else messages[-1]
        for step in far_first
    ]
    pair = jnp.concatenate([tm_message, exchanged(tm_message, "tm", 1)], axis=0)
    pairs = [pair] + [exchanged(pair, "tm", step) for step in range(2, nt, 2)]
    nearest, pairs[-1] = lax.optimization_barrier((nearest, pairs[-1]))
    messages.append(exchanged(nearest, "freq", 1))
    stat_rows = columns // bins + frames // bins
    (stats,) = call(
        totals_kernel, "totals", [((stat_rows, bins), f32)], [], templates, frame_sums
    )
    *arrivals, own_state, clips_wide = call(
        functools.partial(entry_kernel, nt, nf),
        "entry",
        [((3 + stat_rows, bins), f32)] * (nf - 1)
        + [((3, bins), f32), ((1, LANES + frames), f32)],
        [((nt, height, bins), f32), ((nt, 1, bins), f32)],
        place,
        decay,
        init_state[None],
        states,
        stats,
        messages[0],
        *pairs,
        scalars=1,
    )
    arrivals = [exchanged(arrivals[-step], "freq", step) for step in far_first]
    noises = call(
        functools.partial(noise_kernel, nf),
        "noise",
        [((topics, width), f32)] * 4,
        [],
        place,
        gauss_noise,
        uniform_noise,
        boost_count[None],
        scalars=1,
    )
    (halves,) = call(
        functools.partial(halves_kernel, rows),
        "halves",
        [(((nf - 1) * topics // 2, bins), bf16)],
        [],
        noises[0],
        *arrivals,
        *messages,
    )
    halves = exchanged(halves, "tm", 1)
    (normed,) = call(
        functools.partial(normed_kernel, nf),
        "normed",
        [((nf, width, bins), bf16)],
        [((nf * bins // LANES, rows, LANES), f32)] * 2,
        own,
        own_state,
        gains,
        *messages,
        *arrivals,
    )
    packed, tail = call(
        functools.partial(sampler_kernel, nf, piece),
        "sampler",
        [((topics * piece // LANES, LANES), bf16), ((topics, LANES), bf16)],
        [],
        place,
        normed,
        encoder,
        halves,
        *noises,
        *messages,
        scalars=1,
    )
    shares = [exchanged(packed, "freq", step) for step in far_first]
    rim = lax.ppermute(tail, "tm", [(index, index + 1) for index in range(nt - 1)])
    height = columns // nt
    stacked, ratio, sums, bound, *away = call(
        functools.partial(rebuild_kernel, nt, nf),
        "rebuild",
        [((columns, frames), bf16), ((frames, bins), bf16), ((8, frames), f32), ((8, bins), f32)]
        + [((height + 8, bins), f32)] * (nt // 2),
        [((topics, LANES + frames), f32), ((16, columns), bf16), ((bins + 16, frames), f32)],
        place,
        packed,
        rim,
        clips_wide,
        templates,
        spectrum,
        stats,
        *shares,
        *arrivals,
        scalars=1,
    )
    steps = [1 << power for power in range(nf.bit_length() - 1)]
    kept = call(
        functools.partial(kept_kernel, nt),
        "kept",
        [((height, bins), f32)] * (nt // 2),
        [],
        place,
        stacked,
        ratio,
        scalars=1,
    )
    crossed = [exchanged(block, "tm", 1) for block in away]

    def message_of(index, *extra):
        (message,) = call(
            message_kernel,
            "message",
            [((height + 16, bins), f32)],
            [],
            bound,
            kept[index],
            crossed[index],
            *extra,
        )
        return message.astype(jnp.float16)

    def sent(message, pairs):
        return lax.ppermute(message, "tm", pairs).astype(f32)

    log_sum = sums[1:2]
    if nt == 8:
        first = [(lap, lap ^ (2 << (lap & 1))) for lap in range(nt)]
        second = [(lap, lap ^ (4 >> (lap & 1))) for lap in range(nt)]
        carried = sent(message_of(0), first)
        direct, log_sum = lax.optimization_barrier((message_of(1), log_sum))
        parts = [sent(direct, first)]
        log_sum = log_sum + exchanged(log_sum, "freq", steps[0])
        carried, log_sum = lax.optimization_barrier((carried, log_sum))
        parts.append(sent(message_of(2, carried), second))
    else:
        log_sum = log_sum + exchanged(log_sum, "freq", steps[0])
        parts = [
            sent(message_of(step - 1), [(lap, lap ^ (2 * step)) for lap in range(nt)])
            for step in range(1, nt // 2)
        ]
    (result,) = call(
        total_kernel, "total", [((height, bins), f32)], [], kept[-1], crossed[-1], *parts
    )
    for step in steps[1:]:
        log_sum = log_sum + exchanged(log_sum, "freq", step)
    frame_loss = jnp.log(sums[0]) - log_sum[0] / sums[2]
    return (frame_loss, result)


def solution(mesh):
    placed = (
        P("freq", "tm"),
        P("freq"),
        P("freq"),
        P("tm"),
        P(None, "freq"),
        P(None, "tm"),
        P(None, None, "tm"),
        P(),
        P("freq", None),
    )
    return jax.shard_map(
        on_device, mesh=mesh, in_specs=placed, out_specs=(P("tm"), P("tm", "freq")), check_vma=False
    )
```

```python
import functools

import jax
import jax.numpy as jnp
from jax import lax
from jax.experimental import pallas as pl
from jax.experimental.pallas import tpu as pltpu
from jax.sharding import PartitionSpec as P

F = 1024
K = 256
L = 16
TOP_CLIP = 5
TAIL = 16
LANES = 128
VMEM = pl.BlockSpec(memory_space=pltpu.VMEM)
SMEM = pl.BlockSpec(memory_space=pltpu.SMEM)
f32 = jnp.float32
bf16 = jnp.bfloat16


def call(kernel, name, outs, scratch, *args, scalars=0, limit=12 << 20):
    return pl.pallas_call(
        kernel,
        name=name,
        out_shape=[jax.ShapeDtypeStruct(shape, dtype) for shape, dtype in outs],
        in_specs=[SMEM] * scalars + [VMEM] * (len(args) - scalars),
        out_specs=[VMEM] * len(outs),
        scratch_shapes=[pltpu.VMEM(shape, dtype) for shape, dtype in scratch],
        compiler_params=pltpu.CompilerParams(vmem_limit_bytes=limit),
        cost_estimate=pl.CostEstimate(flops=0, bytes_accessed=0, transcendentals=0),
    )(*args)


def log_keep(decay):
    gap = 1.0 - (1.0 - decay)
    series = gap * (1.0 / 7.0)
    for order in range(6, 0, -1):
        series = gap * (1.0 / order + series)
    return -series


def column(row, lanes=LANES):
    return jnp.transpose(jnp.broadcast_to(row, (lanes, row.shape[1])))


def wide(col, lanes):
    return jnp.concatenate([col] * (lanes // col.shape[1]), axis=1)


def steps_down(size):
    return (size - 1 - lax.broadcasted_iota(jnp.int32, (size, 1), 0)).astype(f32)


def pieces_kernel(nf, place, both, small, *refs):
    messages, (own, frame_sums, *summary, frames_first, all_gains) = refs[: nf - 1], refs[nf - 1 :]
    frames, bins = frames_first.shape
    spectrum, encoder = both.at[:, 0:frames], both.at[:, frames:]
    piece = frames // nf
    half = encoder.shape[0] // 2
    here, core = place[0, 0], place[0, 1] & 1
    spectral = spectrum[...].astype(f32)
    turned = jnp.transpose(spectral)
    frames_first[...] = turned
    for step in range(nf):
        target = own if step == 0 else messages[-step]
        start = pl.multiple_of((here ^ step) * piece, piece)
        target[0:piece, :] = frames_first[pl.ds(start, piece), :].astype(bf16)
        target[piece : piece + TAIL, :] = turned[frames - TAIL :].astype(bf16)
        if step:
            low = pl.multiple_of(core * half, half)
            target[piece + TAIL :, :] = encoder[pl.ds(low, half), :]
    total = jnp.sum(spectral, axis=0, keepdims=True)
    for row in range(frames // bins):
        frame_sums[row : row + 1, :] = total[:, row * bins : (row + 1) * bins]
    summarize(nf, place, frames_first, small, *summary, all_gains)


def summarize(nf, place, frames_first, small, gains, states, tm_message, all_gains):
    frames, bins = frames_first.shape
    piece = frames // nf
    here = place[0, 0]
    clip_row = small[:, bins:]
    clip_col = column(clip_row)
    first = clip_row[:, :1]
    gain = jnp.ones_like(clip_col)
    for value in range(1, TOP_CLIP + 1):
        seen = jnp.max(jnp.where(clip_row == value, 1.0, 0.0), axis=1, keepdims=True)
        counts = (seen > 0.0) & (first < value)
        gain = jnp.where(counts & (clip_col >= value), gain * 0.8, gain)
    all_gains[...] = gain
    start = pl.multiple_of(here * piece, piece)
    gains[0:piece, :] = all_gains[pl.ds(start, piece), :]
    gains[piece:, :] = gain[frames - TAIL :]
    rate = small[:, 0:bins]
    keep = log_keep(rate)
    scaled = frames_first[...] * wide(1.0 / gain, bins) * rate
    weights = jnp.exp(steps_down(piece) * keep)
    state = jnp.zeros((1, bins), f32)
    states[...] = jnp.zeros_like(states)
    for index in range(nf):
        states[index : index + 1, :] = state
        rows = scaled[index * piece : (index + 1) * piece]
        if index < nf - 1:
            state = jnp.exp(piece * keep) * state + jnp.sum(rows * weights, axis=0, keepdims=True)
    body = piece - TAIL
    state = jnp.exp(body * keep) * state + jnp.sum(
        rows[:body] * weights[TAIL:], axis=0, keepdims=True
    )
    states[nf : nf + 1, :] = state
    state = jnp.exp(TAIL * keep) * state + jnp.sum(
        rows[body:] * weights[body:], axis=0, keepdims=True
    )
    tm_message[0:1, :] = state
    for row in range(frames // bins):
        tm_message[row + 1 : row + 2, :] = clip_row[:, row * bins : (row + 1) * bins]


def halves_kernel(rows, _, *refs):
    messages = refs[len(refs) // 2 : -1]
    half = messages[0].shape[0] - rows
    for index, message in enumerate(messages):
        refs[-1][index * half : (index + 1) * half, :] = message[rows:, :]


def totals_kernel(templates, frame_sums, stats):
    bins, columns = templates.shape
    for row in range(columns // bins):
        part = templates[:, row * bins : (row + 1) * bins].astype(f32)
        stats[row : row + 1, :] = jnp.sum(part, axis=0, keepdims=True)
    stats[columns // bins : columns // bins + frame_sums.shape[0], :] = frame_sums[...]


def entry_kernel(nt, nf, place, decay, init, states, stats, *refs):
    refs = refs[1:]
    pairs, messages, (own, clips_wide), (blocks, gains) = (
        refs[: nt // 2],
        refs[nt // 2 : nt // 2 + nf - 1],
        refs[nt // 2 + nf - 1 : nt // 2 + nf + 1],
        refs[nt // 2 + nf + 1 :],
    )
    bins = decay.shape[1]
    height = blocks.shape[1]
    frames = (height - 1) * bins
    piece = frames // nf
    here, lap = place[0, 0], place[0, 1]
    for index, pair in enumerate(pairs):
        blocks[2 * index] = pair[0:height]
        blocks[2 * index + 1] = pair[height:]
    ids = blocks[:, 1:, :]
    kinds = jnp.zeros((nt, 1, 1), f32)
    for value in range(TOP_CLIP + 1):
        kinds += jnp.max(jnp.where(ids == value, 1.0, 0.0), axis=(1, 2), keepdims=True)
    gain = jnp.ones_like(kinds)
    for value in range(2, TOP_CLIP + 2):
        gain = jnp.where(kinds >= value, gain * 0.8, gain)
    gains[...] = jnp.broadcast_to(gain, gains.shape)
    keep = log_keep(decay[...])
    through = jnp.exp(frames * keep)
    state = init[...]
    for block in range(nt - 1):
        at, after = block ^ lap, (block + 1) ^ lap
        last = blocks[at, height - 1 : height, bins - 1 : bins]
        first = blocks[after, 1:2, 0:1]
        joint = jnp.where(first != last, 0.8, 1.0)
        passed = joint * (gains[at] * (through * state + blocks[at, 0:1, :]))
        state = jnp.where(block < lap, passed, state)
    tail = jnp.exp((frames - TAIL) * keep) * state + states[nf : nf + 1, :]
    for step in range(nf):
        target = own if step == 0 else messages[-step]
        other = here ^ step
        power = jnp.exp((other * piece).astype(f32) * keep)
        target[0:1, :] = power * state + states[pl.ds(other, 1), :]
        target[1:2, :] = tail
        target[2:3, :] = decay[...]
        if step:
            target[3:, :] = stats[...]
    previous = blocks[jnp.maximum(lap - 1, 0) ^ lap, height - 1 : height, bins - LANES : bins]
    clips_wide[:, 0:LANES] = jnp.where(lap > 0, previous, -1.0)
    for row in range(frames // bins):
        low = LANES + row * bins
        clips_wide[:, low : low + bins] = blocks[0, row + 1 : row + 2, :]


def noise_kernel(nf, place, gauss, uniform, boost, normal, first, second, boosts):
    topics, frames = gauss.shape
    piece = frames // nf
    here = place[0, 0]
    width = normal.shape[1]
    counts = wide(column(boost[...].astype(f32)), width)
    boosts[...] = counts
    normal[...] = jnp.zeros_like(normal)
    first[...] = jnp.ones_like(first)
    second[...] = jnp.ones_like(second)
    pairs = ((gauss, normal), (uniform.at[0], first), (uniform.at[1], second))
    for index in range(nf):

        @pl.when(here == index)
        def _():
            for source, target in pairs:
                target[:, 0:piece] = source[:, index * piece : (index + 1) * piece]

    for source, target in pairs:
        target[:, piece : piece + TAIL] = source[:, frames - TAIL :]
    first[...] = jnp.log(first[...])
    second[...] = jnp.where(counts >= 2.0, jnp.log(second[...]), 0.0)


def normed_kernel(nf, own, own_state, gains, *refs):
    messages, arrivals, (normed, inputs, running) = (
        refs[: nf - 1],
        refs[nf - 1 : 2 * nf - 2],
        refs[2 * nf - 2 :],
    )
    rows, bins = own.shape
    piece = rows - TAIL
    segment = piece // 8
    gain = gains[...]
    inverse = 1.0 / gain
    powers = (1 + lax.broadcasted_iota(jnp.int32, (segment, 1), 0)).astype(f32)
    normed[:, rows:, :] = jnp.zeros_like(normed[:, rows:, :])
    for step in range(nf):
        state = own_state if step == 0 else arrivals[-step]
        block = own if step == 0 else messages[-step]
        for part in range(bins // LANES):
            at = step * (bins // LANES) + part
            lanes = slice(part * LANES, (part + 1) * LANES)
            spectral = block[0:rows, lanes].astype(f32)
            rate = state[2:3, lanes]
            keep = log_keep(rate)
            fade = 1.0 - rate
            inputs[at] = spectral * inverse * rate
            total = jnp.zeros((8, LANES), f32)
            for row in range(segment):
                total = fade * total + inputs[at, pl.ds(row, 8, stride=segment), :]
                running[at, pl.ds(row, 8, stride=segment), :] = total
            carry = state[0:1, lanes]
            through = jnp.exp(segment * keep)
            fading = jnp.exp(powers * keep)
            for index in range(8):
                low = index * segment
                running[at, low : low + segment, :] += fading * carry
                carry = through * carry + total[index : index + 1, :]
            carry = state[1:2, lanes]
            for row in range(piece, rows):
                carry = fade * carry + inputs[at, row : row + 1, :]
                running[at, row : row + 1, :] = carry
            smooth = running[at] * gain
            normed[step, 0:rows, lanes] = (spectral * lax.rsqrt(smooth + 0.1)).astype(bf16)


def sampler_kernel(nf, piece, place, normed, encoder, halves, normal, first, second, boosts, *refs):
    messages, (packed, tail) = refs[: nf - 1], refs[nf - 1 :]
    core = place[0, 1] & 1
    topics, width = normal.shape
    half = topics // 2
    rows = piece + TAIL
    logits = jnp.zeros((topics, width), f32)
    for step in range(nf):
        if step == 0:
            weights = encoder[...]
        else:
            mine = messages[-step][rows:, :]
            other = halves[(nf - 1 - step) * half : (nf - step) * half, :]
            lower = jnp.where(core == 0, mine, other)
            upper = jnp.where(core == 0, other, mine)
            weights = jnp.concatenate([lower, upper], axis=0)
        logits += lax.dot_general(
            weights, normed[step], (((1,), (1,)), ((), ())), preferred_element_type=f32
        )
    concentration = jnp.maximum(logits, 0.0) + jnp.log1p(jnp.exp(-jnp.abs(logits))) + 0.5
    offset = concentration + boosts[...] - 1.0 / 3.0
    linear = 1.0 + lax.rsqrt(9.0 * offset) * normal[...]
    draw = offset * linear * linear * linear
    draw = draw * jnp.exp(first[...] / concentration + second[...] / (concentration + 1.0))
    proportions = draw / jnp.sum(draw, axis=0, keepdims=True)
    full, rest = piece // LANES, piece % LANES
    for index in range(full):
        tile = proportions[:, index * LANES : (index + 1) * LANES]
        packed[index * topics : (index + 1) * topics, :] = tile.astype(bf16)
    tile = proportions[:, full * LANES : (full + 1) * LANES]
    if rest:
        lane = lax.broadcasted_iota(jnp.int32, (half, LANES), 1)
        joined = jnp.where(lane < rest, tile[:half], pltpu.roll(tile[half:], rest, 1))
        packed[full * topics :, :] = joined.astype(bf16)
    tail[...] = pltpu.roll(tile, LANES - TAIL - rest, 1).astype(bf16)


def rebuild_kernel(nt, nf, place, own, rim, clips, templates, spectrum, stats, *refs):
    messages, arrivals, (stacked, ratio, sums, bound, *away, extended, heads, recon) = (
        refs[: nf - 1],
        refs[nf - 1 : 2 * nf - 2],
        refs[2 * nf - 2 :],
    )
    bins, frames = spectrum.shape
    here = place[0, 0]
    piece = frames // nf
    topics = extended.shape[0]
    full, rest = piece // LANES, piece % LANES
    extended[:, 0:LANES] = rim[...].astype(f32)
    for step in range(nf):
        source = own if step == 0 else messages[-step]
        for index in range(nf):

            @pl.when((here ^ step) == index)
            def _():
                low = LANES + index * piece
                for part in range(full):
                    values = source[part * topics : (part + 1) * topics, :].astype(f32)
                    extended[:, low + part * LANES : low + (part + 1) * LANES] = values
                if rest:
                    values = source[full * topics :, :].astype(f32)
                    low += full * LANES
                    half = topics // 2
                    extended[0:half, low : low + rest] = values[:, 0:rest]
                    extended[half:, low : low + rest] = values[:, rest:]

    total = stats[...]
    for arrival in arrivals:
        total = total + arrival[3:, :]
    columns = templates.shape[1]
    wide_rows = columns // bins
    heads[...] = jnp.zeros_like(heads)
    for row in range(wide_rows):
        value = total[row : row + 1, :]
        for index in range(3):
            rounded = value.astype(bf16)
            heads[index : index + 1, row * bins : (row + 1) * bins] = rounded
            value = value - rounded.astype(f32)
    for row in range(frames // bins):
        at = wide_rows + row
        sums[2:3, row * bins : (row + 1) * bins] = total[at : at + 1, :]
    ids = jnp.broadcast_to(clips[...], (L, LANES + frames))
    shifted = pltpu.roll(ids, 0, 1, stride=1, stride_axis=0)
    valid = jnp.where(shifted == ids, 1.0, 0.0)[:, LANES:].astype(bf16)
    group = 32
    for low in range(0, topics, group):
        for topic in range(low, low + group):
            row = jnp.broadcast_to(extended[topic : topic + 1, :], (L, LANES + frames))
            lagged = pltpu.roll(row, 0, 1, stride=1, stride_axis=0)[:, LANES:]
            stacked[topic * L : (topic + 1) * L, :] = lagged.astype(bf16) * valid
        part = slice(low * L, (low + group) * L)
        left = jnp.concatenate([templates[:, part], heads[:, part]], axis=0)
        product = jnp.dot(left, stacked[part, :], preferred_element_type=f32)
        if low == 0:
            recon[...] = product
        else:
            recon[...] += product
    rebuilt = recon[0:bins, :]
    recon_sum = recon[bins : bins + 1] + recon[bins + 1 : bins + 2] + recon[bins + 2 : bins + 3]
    spectral = spectrum[...].astype(f32)
    scale = F * K / (frames * nt)
    rounded = (scale * (1.0 / recon_sum - spectral / (sums[2:3, :] * rebuilt))).astype(bf16)
    turned = jnp.transpose(rounded.astype(f32))
    ratio[...] = turned.astype(bf16)
    reach = jnp.sum(jnp.abs(turned), axis=0, keepdims=True)
    bound[...] = jnp.broadcast_to(jnp.max(reach, axis=1, keepdims=True), bound.shape)
    sums[0:1, :] = recon_sum
    sums[1:2, :] = jnp.sum(spectral * jnp.log(rebuilt), axis=0, keepdims=True)
    products(1, nt, place, stacked, ratio, away)
    for target in away:
        target[target.shape[0] - 8 :, :] = bound[...]


def products(side, nt, place, stacked, ratio, targets):
    height = stacked.shape[0] // nt
    lap = place[0, 1]
    hop = 1 + ((lap ^ side) & 1)
    order = (3, hop, 3 ^ hop, 0) if nt == 8 else (*range(1, len(targets)), 0)
    for step, target in zip(order, targets):
        at = pl.multiple_of((lap ^ (2 * step + side)) * height, height)
        target[0:height, :] = jnp.dot(
            stacked[pl.ds(at, height), :], ratio[...], preferred_element_type=f32
        )


def kept_kernel(nt, place, stacked, ratio, *targets):
    products(0, nt, place, stacked, ratio, targets)


def message_kernel(bound, kept, crossed, *refs):
    parts, message = refs[:-1], refs[-1]
    height = kept.shape[0]
    limit = bound[0:1, :] + crossed[height : height + 1, :]
    value = kept[...] + crossed[0:height, :]
    for part in parts:
        carried = part[height : height + 1, :]
        limit = limit + carried * 32768.0
        value = value + part[0:height, :] * carried
    unit = jnp.maximum(limit * (1.02 / 32768.0), 2.0**-14).astype(bf16).astype(f32)
    message[0:height, :] = value * (1.0 / unit)
    message[height:, :] = jnp.broadcast_to(unit, (16, kept.shape[1]))


def total_kernel(kept, crossed, *refs):
    parts, total = refs[:-1], refs[-1]
    height = kept.shape[0]
    value = kept[...] + crossed[0:height, :]
    for part in parts:
        value = value + part[0:height, :] * part[height : height + 1, :]
    total[...] = value


def exchanged(value, axis, step):
    size = lax.axis_size(axis)
    return lax.ppermute(value, axis, [(index, index ^ step) for index in range(size)])


def on_device(
    spectrum,
    decay_rate,
    init_state,
    clip_ids,
    encoder,
    gauss_noise,
    uniform_noise,
    boost_count,
    templates,
):
    nt, nf = lax.axis_size("tm"), lax.axis_size("freq")
    bins, frames = spectrum.shape
    topics = encoder.shape[0]
    columns = templates.shape[1]
    piece = frames // nf
    rows = piece + TAIL
    width = -(-rows // LANES) * LANES
    far_first = range(nf - 1, 0, -1)
    place = jnp.stack([lax.axis_index("freq"), lax.axis_index("tm")]).astype(jnp.int32)[None]
    decay = decay_rate[None]
    state_rows = -(-(nf + 1) // 8) * 8
    height = 1 + frames // bins

    small = jnp.pad(decay_rate, (0, frames)) + jnp.pad(clip_ids, (bins, 0)).astype(f32)
    *messages, own, frame_sums, gains, states, tm_message = call(
        functools.partial(pieces_kernel, nf),
        "pieces",
        [((rows + topics // 2, bins), bf16)] * (nf - 1)
        + [((rows, bins), bf16), ((frames // bins, bins), f32), ((rows, LANES), f32)]
        + [((state_rows, bins), f32), ((height, bins), f32)],
        [((frames, bins), f32), ((frames, LANES), f32)],
        place,
        jnp.concatenate([spectrum, encoder], axis=1),
        small[None],
        scalars=1,
    )
    *messages, nearest = [
        exchanged(messages[-step], "freq", step) if step > 1 else messages[-1]
        for step in far_first
    ]
    pair = jnp.concatenate([tm_message, exchanged(tm_message, "tm", 1)], axis=0)
    pairs = [pair] + [exchanged(pair, "tm", step) for step in range(2, nt, 2)]
    nearest, pairs[-1] = lax.optimization_barrier((nearest, pairs[-1]))
    messages.append(exchanged(nearest, "freq", 1))
    stat_rows = columns // bins + frames // bins
    (stats,) = call(
        totals_kernel, "totals", [((stat_rows, bins), f32)], [], templates, frame_sums
    )
    *arrivals, own_state, clips_wide = call(
        functools.partial(entry_kernel, nt, nf),
        "entry",
        [((3 + stat_rows, bins), f32)] * (nf - 1)
        + [((3, bins), f32), ((1, LANES + frames), f32)],
        [((nt, height, bins), f32), ((nt, 1, bins), f32)],
        place,
        decay,
        init_state[None],
        states,
        stats,
        messages[0],
        *pairs,
        scalars=1,
    )
    arrivals = [exchanged(arrivals[-step], "freq", step) for step in far_first]
    noises = call(
        functools.partial(noise_kernel, nf),
        "noise",
        [((topics, width), f32)] * 4,
        [],
        place,
        gauss_noise,
        uniform_noise,
        boost_count[None],
        scalars=1,
    )
    (halves,) = call(
        functools.partial(halves_kernel, rows),
        "halves",
        [(((nf - 1) * topics // 2, bins), bf16)],
        [],
        noises[0],
        *arrivals,
        *messages,
    )
    halves = exchanged(halves, "tm", 1)
    (normed,) = call(
        functools.partial(normed_kernel, nf),
        "normed",
        [((nf, width, bins), bf16)],
        [((nf * bins // LANES, rows, LANES), f32)] * 2,
        own,
        own_state,
        gains,
        *messages,
        *arrivals,
    )
    packed, tail = call(
        functools.partial(sampler_kernel, nf, piece),
        "sampler",
        [((topics * piece // LANES, LANES), bf16), ((topics, LANES), bf16)],
        [],
        place,
        normed,
        encoder,
        halves,
        *noises,
        *messages,
        scalars=1,
    )
    shares = [exchanged(packed, "freq", step) for step in far_first]
    rim = lax.ppermute(tail, "tm", [(index, index + 1) for index in range(nt - 1)])
    height = columns // nt
    stacked, ratio, sums, bound, *away = call(
        functools.partial(rebuild_kernel, nt, nf),
        "rebuild",
        [((columns, frames), bf16), ((frames, bins), bf16), ((8, frames), f32), ((8, bins), f32)]
        + [((height + 8, bins), f32)] * (nt // 2),
        [((topics, LANES + frames), f32), ((16, columns), bf16), ((bins + 16, frames), f32)],
        place,
        packed,
        rim,
        clips_wide,
        templates,
        spectrum,
        stats,
        *shares,
        *arrivals,
        scalars=1,
    )
    steps = [1 << power for power in range(nf.bit_length() - 1)]
    kept = call(
        functools.partial(kept_kernel, nt),
        "kept",
        [((height, bins), f32)] * (nt // 2),
        [],
        place,
        stacked,
        ratio,
        scalars=1,
    )
    crossed = [exchanged(block, "tm", 1) for block in away]

    def message_of(index, *extra):
        (message,) = call(
            message_kernel,
            "message",
            [((height + 16, bins), f32)],
            [],
            bound,
            kept[index],
            crossed[index],
            *extra,
        )
        return message.astype(jnp.float16)

    def sent(message, pairs):
        return lax.ppermute(message, "tm", pairs).astype(f32)

    log_sum = sums[1:2]
    if nt == 8:
        first = [(lap, lap ^ (2 << (lap & 1))) for lap in range(nt)]
        second = [(lap, lap ^ (4 >> (lap & 1))) for lap in range(nt)]
        carried = sent(message_of(0), first)
        direct, log_sum = lax.optimization_barrier((message_of(1), log_sum))
        parts = [sent(direct, first)]
        log_sum = log_sum + exchanged(log_sum, "freq", steps[0])
        carried, log_sum = lax.optimization_barrier((carried, log_sum))
        parts.append(sent(message_of(2, carried), second))
    else:
        log_sum = log_sum + exchanged(log_sum, "freq", steps[0])
        parts = [
            sent(message_of(step - 1), [(lap, lap ^ (2 * step)) for lap in range(nt)])
            for step in range(1, nt // 2)
        ]
    (result,) = call(
        total_kernel, "total", [((height, bins), f32)], [], kept[-1], crossed[-1], *parts
    )
    for step in steps[1:]:
        log_sum = log_sum + exchanged(log_sum, "freq", step)
    frame_loss = jnp.log(sums[0]) - log_sum[0] / sums[2]
    return (frame_loss, result)


def solution(mesh):
    placed = (
        P("freq", "tm"),
        P("freq"),
        P("freq"),
        P("tm"),
        P(None, "freq"),
        P(None, "tm"),
        P(None, None, "tm"),
        P(),
        P("freq", None),
    )
    return jax.shard_map(
        on_device, mesh=mesh, in_specs=placed, out_specs=(P("tm"), P("tm", "freq")), check_vma=False
    )
```

```python
import functools

import jax
import jax.numpy as jnp
from jax import lax
from jax.experimental import pallas as pl
from jax.experimental.pallas import tpu as pltpu
from jax.sharding import PartitionSpec as P

F = 1024
K = 256
L = 16
TOP_CLIP = 5
TAIL = 16
LANES = 128
VMEM = pl.BlockSpec(memory_space=pltpu.VMEM)
SMEM = pl.BlockSpec(memory_space=pltpu.SMEM)
f32 = jnp.float32
bf16 = jnp.bfloat16


def call(kernel, name, outs, scratch, *args, scalars=0, limit=12 << 20):
    return pl.pallas_call(
        kernel,
        name=name,
        out_shape=[jax.ShapeDtypeStruct(shape, dtype) for shape, dtype in outs],
        in_specs=[SMEM] * scalars + [VMEM] * (len(args) - scalars),
        out_specs=[VMEM] * len(outs),
        scratch_shapes=[pltpu.VMEM(shape, dtype) for shape, dtype in scratch],
        compiler_params=pltpu.CompilerParams(vmem_limit_bytes=limit),
        cost_estimate=pl.CostEstimate(flops=0, bytes_accessed=0, transcendentals=0),
    )(*args)


def log_keep(decay):
    gap = 1.0 - (1.0 - decay)
    series = gap * (1.0 / 7.0)
    for order in range(6, 0, -1):
        series = gap * (1.0 / order + series)
    return -series


def column(row, lanes=LANES):
    return jnp.transpose(jnp.broadcast_to(row, (lanes, row.shape[1])))


def wide(col, lanes):
    return jnp.concatenate([col] * (lanes // col.shape[1]), axis=1)


def steps_down(size):
    return (size - 1 - lax.broadcasted_iota(jnp.int32, (size, 1), 0)).astype(f32)


def pieces_kernel(nf, place, both, small, *refs):
    messages, (own, frame_sums, *summary, frames_first, all_gains) = refs[: nf - 1], refs[nf - 1 :]
    frames, bins = frames_first.shape
    spectrum, encoder = both.at[:, 0:frames], both.at[:, frames:]
    piece = frames // nf
    half = encoder.shape[0] // 2
    here, core = place[0, 0], place[0, 1] & 1
    spectral = spectrum[...].astype(f32)
    turned = jnp.transpose(spectral)
    frames_first[...] = turned
    for step in range(nf):
        target = own if step == 0 else messages[-step]
        start = pl.multiple_of((here ^ step) * piece, piece)
        target[0:piece, :] = frames_first[pl.ds(start, piece), :].astype(bf16)
        target[piece : piece + TAIL, :] = turned[frames - TAIL :].astype(bf16)
        if step:
            low = pl.multiple_of(core * half, half)
            target[piece + TAIL :, :] = encoder[pl.ds(low, half), :]
    total = jnp.sum(spectral, axis=0, keepdims=True)
    for row in range(frames // bins):
        frame_sums[row : row + 1, :] = total[:, row * bins : (row + 1) * bins]
    summarize(nf, place, frames_first, small, *summary, all_gains)


def summarize(nf, place, frames_first, small, gains, states, tm_message, all_gains):
    frames, bins = frames_first.shape
    piece = frames // nf
    here = place[0, 0]
    clip_row = small[:, bins:]
    clip_col = column(clip_row)
    first = clip_row[:, :1]
    gain = jnp.ones_like(clip_col)
    for value in range(1, TOP_CLIP + 1):
        seen = jnp.max(jnp.where(clip_row == value, 1.0, 0.0), axis=1, keepdims=True)
        counts = (seen > 0.0) & (first < value)
        gain = jnp.where(counts & (clip_col >= value), gain * 0.8, gain)
    all_gains[...] = gain
    start = pl.multiple_of(here * piece, piece)
    gains[0:piece, :] = all_gains[pl.ds(start, piece), :]
    gains[piece:, :] = gain[frames - TAIL :]
    rate = small[:, 0:bins]
    keep = log_keep(rate)
    scaled = frames_first[...] * wide(1.0 / gain, bins) * rate
    weights = jnp.exp(steps_down(piece) * keep)
    state = jnp.zeros((1, bins), f32)
    states[...] = jnp.zeros_like(states)
    for index in range(nf):
        states[index : index + 1, :] = state
        rows = scaled[index * piece : (index + 1) * piece]
        if index < nf - 1:
            state = jnp.exp(piece * keep) * state + jnp.sum(rows * weights, axis=0, keepdims=True)
    body = piece - TAIL
    state = jnp.exp(body * keep) * state + jnp.sum(
        rows[:body] * weights[TAIL:], axis=0, keepdims=True
    )
    states[nf : nf + 1, :] = state
    state = jnp.exp(TAIL * keep) * state + jnp.sum(
        rows[body:] * weights[body:], axis=0, keepdims=True
    )
    tm_message[0:1, :] = state
    for row in range(frames // bins):
        tm_message[row + 1 : row + 2, :] = clip_row[:, row * bins : (row + 1) * bins]


def halves_kernel(rows, _, *refs):
    messages = refs[len(refs) // 2 : -1]
    half = messages[0].shape[0] - rows
    for index, message in enumerate(messages):
        refs[-1][index * half : (index + 1) * half, :] = message[rows:, :]


def totals_kernel(templates, frame_sums, stats):
    bins, columns = templates.shape
    for row in range(columns // bins):
        part = templates[:, row * bins : (row + 1) * bins].astype(f32)
        stats[row : row + 1, :] = jnp.sum(part, axis=0, keepdims=True)
    stats[columns // bins : columns // bins + frame_sums.shape[0], :] = frame_sums[...]


def entry_kernel(nt, nf, place, decay, init, states, stats, *refs):
    refs = refs[1:]
    pairs, messages, (own, clips_wide), (blocks, gains) = (
        refs[: nt // 2],
        refs[nt // 2 : nt // 2 + nf - 1],
        refs[nt // 2 + nf - 1 : nt // 2 + nf + 1],
        refs[nt // 2 + nf + 1 :],
    )
    bins = decay.shape[1]
    height = blocks.shape[1]
    frames = (height - 1) * bins
    piece = frames // nf
    here, lap = place[0, 0], place[0, 1]
    for index, pair in enumerate(pairs):
        blocks[2 * index] = pair[0:height]
        blocks[2 * index + 1] = pair[height:]
    ids = blocks[:, 1:, :]
    kinds = jnp.zeros((nt, 1, 1), f32)
    for value in range(TOP_CLIP + 1):
        kinds += jnp.max(jnp.where(ids == value, 1.0, 0.0), axis=(1, 2), keepdims=True)
    gain = jnp.ones_like(kinds)
    for value in range(2, TOP_CLIP + 2):
        gain = jnp.where(kinds >= value, gain * 0.8, gain)
    gains[...] = jnp.broadcast_to(gain, gains.shape)
    keep = log_keep(decay[...])
    through = jnp.exp(frames * keep)
    state = init[...]
    for block in range(nt - 1):
        at, after = block ^ lap, (block + 1) ^ lap
        last = blocks[at, height - 1 : height, bins - 1 : bins]
        first = blocks[after, 1:2, 0:1]
        joint = jnp.where(first != last, 0.8, 1.0)
        passed = joint * (gains[at] * (through * state + blocks[at, 0:1, :]))
        state = jnp.where(block < lap, passed, state)
    tail = jnp.exp((frames - TAIL) * keep) * state + states[nf : nf + 1, :]
    for step in range(nf):
        target = own if step == 0 else messages[-step]
        other = here ^ step
        power = jnp.exp((other * piece).astype(f32) * keep)
        target[0:1, :] = power * state + states[pl.ds(other, 1), :]
        target[1:2, :] = tail
        target[2:3, :] = decay[...]
        if step:
            target[3:, :] = stats[...]
    previous = blocks[jnp.maximum(lap - 1, 0) ^ lap, height - 1 : height, bins - LANES : bins]
    clips_wide[:, 0:LANES] = jnp.where(lap > 0, previous, -1.0)
    for row in range(frames // bins):
        low = LANES + row * bins
        clips_wide[:, low : low + bins] = blocks[0, row + 1 : row + 2, :]


def noise_kernel(nf, place, gauss, uniform, boost, normal, first, second, boosts):
    topics, frames = gauss.shape
    piece = frames // nf
    here = place[0, 0]
    width = normal.shape[1]
    counts = wide(column(boost[...].astype(f32)), width)
    boosts[...] = counts
    normal[...] = jnp.zeros_like(normal)
    first[...] = jnp.ones_like(first)
    second[...] = jnp.ones_like(second)
    pairs = ((gauss, normal), (uniform.at[0], first), (uniform.at[1], second))
    for index in range(nf):

        @pl.when(here == index)
        def _():
            for source, target in pairs:
                target[:, 0:piece] = source[:, index * piece : (index + 1) * piece]

    for source, target in pairs:
        target[:, piece : piece + TAIL] = source[:, frames - TAIL :]
    first[...] = jnp.log(first[...])
    second[...] = jnp.where(counts >= 2.0, jnp.log(second[...]), 0.0)


def normed_kernel(nf, own, own_state, gains, *refs):
    messages, arrivals, (normed, inputs, running) = (
        refs[: nf - 1],
        refs[nf - 1 : 2 * nf - 2],
        refs[2 * nf - 2 :],
    )
    rows, bins = own.shape
    piece = rows - TAIL
    segment = piece // 8
    gain = gains[...]
    inverse = 1.0 / gain
    powers = (1 + lax.broadcasted_iota(jnp.int32, (segment, 1), 0)).astype(f32)
    normed[:, rows:, :] = jnp.zeros_like(normed[:, rows:, :])
    for step in range(nf):
        state = own_state if step == 0 else arrivals[-step]
        block = own if step == 0 else messages[-step]
        for part in range(bins // LANES):
            at = step * (bins // LANES) + part
            lanes = slice(part * LANES, (part + 1) * LANES)
            spectral = block[0:rows, lanes].astype(f32)
            rate = state[2:3, lanes]
            keep = log_keep(rate)
            fade = 1.0 - rate
            inputs[at] = spectral * inverse * rate
            total = jnp.zeros((8, LANES), f32)
            for row in range(segment):
                total = fade * total + inputs[at, pl.ds(row, 8, stride=segment), :]
                running[at, pl.ds(row, 8, stride=segment), :] = total
            carry = state[0:1, lanes]
            through = jnp.exp(segment * keep)
            fading = jnp.exp(powers * keep)
            for index in range(8):
                low = index * segment
                running[at, low : low + segment, :] += fading * carry
                carry = through * carry + total[index : index + 1, :]
            carry = state[1:2, lanes]
            for row in range(piece, rows):
                carry = fade * carry + inputs[at, row : row + 1, :]
                running[at, row : row + 1, :] = carry
            smooth = running[at] * gain
            normed[step, 0:rows, lanes] = (spectral * lax.rsqrt(smooth + 0.1)).astype(bf16)


def sampler_kernel(nf, piece, place, normed, encoder, halves, normal, first, second, boosts, *refs):
    messages, (packed, tail) = refs[: nf - 1], refs[nf - 1 :]
    core = place[0, 1] & 1
    topics, width = normal.shape
    half = topics // 2
    rows = piece + TAIL
    logits = jnp.zeros((topics, width), f32)
    for step in range(nf):
        if step == 0:
            weights = encoder[...]
        else:
            mine = messages[-step][rows:, :]
            other = halves[(nf - 1 - step) * half : (nf - step) * half, :]
            lower = jnp.where(core == 0, mine, other)
            upper = jnp.where(core == 0, other, mine)
            weights = jnp.concatenate([lower, upper], axis=0)
        logits += lax.dot_general(
            weights, normed[step], (((1,), (1,)), ((), ())), preferred_element_type=f32
        )
    concentration = jnp.maximum(logits, 0.0) + jnp.log1p(jnp.exp(-jnp.abs(logits))) + 0.5
    offset = concentration + boosts[...] - 1.0 / 3.0
    linear = 1.0 + lax.rsqrt(9.0 * offset) * normal[...]
    draw = offset * linear * linear * linear
    draw = draw * jnp.exp(first[...] / concentration + second[...] / (concentration + 1.0))
    proportions = draw / jnp.sum(draw, axis=0, keepdims=True)
    full, rest = piece // LANES, piece % LANES
    for index in range(full):
        tile = proportions[:, index * LANES : (index + 1) * LANES]
        packed[index * topics : (index + 1) * topics, :] = tile.astype(bf16)
    tile = proportions[:, full * LANES : (full + 1) * LANES]
    if rest:
        lane = lax.broadcasted_iota(jnp.int32, (half, LANES), 1)
        joined = jnp.where(lane < rest, tile[:half], pltpu.roll(tile[half:], rest, 1))
        packed[full * topics :, :] = joined.astype(bf16)
    tail[...] = pltpu.roll(tile, LANES - TAIL - rest, 1).astype(bf16)


def rebuild_kernel(nt, nf, place, own, rim, clips, templates, spectrum, stats, *refs):
    messages, arrivals, (stacked, ratio, sums, bound, *away, extended, heads, recon) = (
        refs[: nf - 1],
        refs[nf - 1 : 2 * nf - 2],
        refs[2 * nf - 2 :],
    )
    bins, frames = spectrum.shape
    here = place[0, 0]
    piece = frames // nf
    topics = extended.shape[0]
    full, rest = piece // LANES, piece % LANES
    extended[:, 0:LANES] = rim[...].astype(f32)
    for step in range(nf):
        source = own if step == 0 else messages[-step]
        for index in range(nf):

            @pl.when((here ^ step) == index)
            def _():
                low = LANES + index * piece
                for part in range(full):
                    values = source[part * topics : (part + 1) * topics, :].astype(f32)
                    extended[:, low + part * LANES : low + (part + 1) * LANES] = values
                if rest:
                    values = source[full * topics :, :].astype(f32)
                    low += full * LANES
                    half = topics // 2
                    extended[0:half, low : low + rest] = values[:, 0:rest]
                    extended[half:, low : low + rest] = values[:, rest:]

    total = stats[...]
    for arrival in arrivals:
        total = total + arrival[3:, :]
    columns = templates.shape[1]
    wide_rows = columns // bins
    heads[...] = jnp.zeros_like(heads)
    for row in range(wide_rows):
        value = total[row : row + 1, :]
        for index in range(3):
            rounded = value.astype(bf16)
            heads[index : index + 1, row * bins : (row + 1) * bins] = rounded
            value = value - rounded.astype(f32)
    for row in range(frames // bins):
        at = wide_rows + row
        sums[2:3, row * bins : (row + 1) * bins] = total[at : at + 1, :]
    ids = jnp.broadcast_to(clips[...], (L, LANES + frames))
    shifted = pltpu.roll(ids, 0, 1, stride=1, stride_axis=0)
    valid = jnp.where(shifted == ids, 1.0, 0.0)[:, LANES:].astype(bf16)
    group = 32
    for low in range(0, topics, group):
        for topic in range(low, low + group):
            row = jnp.broadcast_to(extended[topic : topic + 1, :], (L, LANES + frames))
            lagged = pltpu.roll(row, 0, 1, stride=1, stride_axis=0)[:, LANES:]
            stacked[topic * L : (topic + 1) * L, :] = lagged.astype(bf16) * valid
        part = slice(low * L, (low + group) * L)
        left = jnp.concatenate([templates[:, part], heads[:, part]], axis=0)
        product = jnp.dot(left, stacked[part, :], preferred_element_type=f32)
        if low == 0:
            recon[...] = product
        else:
            recon[...] += product
    rebuilt = recon[0:bins, :]
    recon_sum = recon[bins : bins + 1] + recon[bins + 1 : bins + 2] + recon[bins + 2 : bins + 3]
    spectral = spectrum[...].astype(f32)
    scale = F * K / (frames * nt)
    rounded = (scale * (1.0 / recon_sum - spectral / (sums[2:3, :] * rebuilt))).astype(bf16)
    turned = jnp.transpose(rounded.astype(f32))
    ratio[...] = turned.astype(bf16)
    reach = jnp.sum(jnp.abs(turned), axis=0, keepdims=True)
    bound[...] = jnp.broadcast_to(jnp.max(reach, axis=1, keepdims=True), bound.shape)
    sums[0:1, :] = recon_sum
    sums[1:2, :] = jnp.sum(spectral * jnp.log(rebuilt), axis=0, keepdims=True)
    products(1, nt, place, stacked, ratio, away)
    for target in away:
        target[target.shape[0] - 8 :, :] = bound[...]


def products(side, nt, place, stacked, ratio, targets):
    height = stacked.shape[0] // nt
    lap = place[0, 1]
    hop = 1 + ((lap ^ side) & 1)
    order = (3, hop, 3 ^ hop, 0) if nt == 8 else (*range(1, len(targets)), 0)
    for step, target in zip(order, targets):
        at = pl.multiple_of((lap ^ (2 * step + side)) * height, height)
        target[0:height, :] = jnp.dot(
            stacked[pl.ds(at, height), :], ratio[...], preferred_element_type=f32
        )


def kept_kernel(nt, place, stacked, ratio, *targets):
    products(0, nt, place, stacked, ratio, targets)


def message_kernel(bound, kept, crossed, *refs):
    parts, message = refs[:-1], refs[-1]
    height = kept.shape[0]
    limit = bound[0:1, :] + crossed[height : height + 1, :]
    value = kept[...] + crossed[0:height, :]
    for part in parts:
        carried = part[height : height + 1, :]
        limit = limit + carried * 32768.0
        value = value + part[0:height, :] * carried
    unit = jnp.maximum(limit * (1.02 / 32768.0), 2.0**-14).astype(bf16).astype(f32)
    message[0:height, :] = value * (1.0 / unit)
    message[height:, :] = jnp.broadcast_to(unit, (16, kept.shape[1]))


def total_kernel(kept, crossed, *refs):
    parts, total = refs[:-1], refs[-1]
    height = kept.shape[0]
    value = kept[...] + crossed[0:height, :]
    for part in parts:
        value = value + part[0:height, :] * part[height : height + 1, :]
    total[...] = value


def exchanged(value, axis, step):
    size = lax.axis_size(axis)
    return lax.ppermute(value, axis, [(index, index ^ step) for index in range(size)])


def on_device(
    spectrum,
    decay_rate,
    init_state,
    clip_ids,
    encoder,
    gauss_noise,
    uniform_noise,
    boost_count,
    templates,
):
    nt, nf = lax.axis_size("tm"), lax.axis_size("freq")
    bins, frames = spectrum.shape
    topics = encoder.shape[0]
    columns = templates.shape[1]
    piece = frames // nf
    rows = piece + TAIL
    width = -(-rows // LANES) * LANES
    far_first = range(nf - 1, 0, -1)
    place = jnp.stack([lax.axis_index("freq"), lax.axis_index("tm")]).astype(jnp.int32)[None]
    decay = decay_rate[None]
    state_rows = -(-(nf + 1) // 8) * 8
    height = 1 + frames // bins

    small = jnp.pad(decay_rate, (0, frames)) + jnp.pad(clip_ids, (bins, 0)).astype(f32)
    *messages, own, frame_sums, gains, states, tm_message = call(
        functools.partial(pieces_kernel, nf),
        "pieces",
        [((rows + topics // 2, bins), bf16)] * (nf - 1)
        + [((rows, bins), bf16), ((frames // bins, bins), f32), ((rows, LANES), f32)]
        + [((state_rows, bins), f32), ((height, bins), f32)],
        [((frames, bins), f32), ((frames, LANES), f32)],
        place,
        jnp.concatenate([spectrum, encoder], axis=1),
        small[None],
        scalars=1,
    )
    *messages, nearest = [
        exchanged(messages[-step], "freq", step) if step > 1 else messages[-1]
        for step in far_first
    ]
    pair = jnp.concatenate([tm_message, exchanged(tm_message, "tm", 1)], axis=0)
    pairs = [pair] + [exchanged(pair, "tm", step) for step in range(2, nt, 2)]
    nearest, *pairs[1:] = lax.optimization_barrier((nearest, *pairs[1:]))
    messages.append(exchanged(nearest, "freq", 1))
    stat_rows = columns // bins + frames // bins
    (stats,) = call(
        totals_kernel, "totals", [((stat_rows, bins), f32)], [], templates, frame_sums
    )
    *arrivals, own_state, clips_wide = call(
        functools.partial(entry_kernel, nt, nf),
        "entry",
        [((3 + stat_rows, bins), f32)] * (nf - 1)
        + [((3, bins), f32), ((1, LANES + frames), f32)],
        [((nt, height, bins), f32), ((nt, 1, bins), f32)],
        place,
        decay,
        init_state[None],
        states,
        stats,
        messages[0],
        *pairs,
        scalars=1,
    )
    arrivals = [exchanged(arrivals[-step], "freq", step) for step in far_first]
    noises = call(
        functools.partial(noise_kernel, nf),
        "noise",
        [((topics, width), f32)] * 4,
        [],
        place,
        gauss_noise,
        uniform_noise,
        boost_count[None],
        scalars=1,
    )
    (halves,) = call(
        functools.partial(halves_kernel, rows),
        "halves",
        [(((nf - 1) * topics // 2, bins), bf16)],
        [],
        noises[0],
        *arrivals,
        *messages,
    )
    halves = exchanged(halves, "tm", 1)
    (normed,) = call(
        functools.partial(normed_kernel, nf),
        "normed",
        [((nf, width, bins), bf16)],
        [((nf * bins // LANES, rows, LANES), f32)] * 2,
        own,
        own_state,
        gains,
        *messages,
        *arrivals,
    )
    packed, tail = call(
        functools.partial(sampler_kernel, nf, piece),
        "sampler",
        [((topics * piece // LANES, LANES), bf16), ((topics, LANES), bf16)],
        [],
        place,
        normed,
        encoder,
        halves,
        *noises,
        *messages,
        scalars=1,
    )
    shares = [exchanged(packed, "freq", step) for step in far_first]
    rim = lax.ppermute(tail, "tm", [(index, index + 1) for index in range(nt - 1)])
    height = columns // nt
    stacked, ratio, sums, bound, *away = call(
        functools.partial(rebuild_kernel, nt, nf),
        "rebuild",
        [((columns, frames), bf16), ((frames, bins), bf16), ((8, frames), f32), ((8, bins), f32)]
        + [((height + 8, bins), f32)] * (nt // 2),
        [((topics, LANES + frames), f32), ((16, columns), bf16), ((bins + 16, frames), f32)],
        place,
        packed,
        rim,
        clips_wide,
        templates,
        spectrum,
        stats,
        *shares,
        *arrivals,
        scalars=1,
    )
    steps = [1 << power for power in range(nf.bit_length() - 1)]
    kept = call(
        functools.partial(kept_kernel, nt),
        "kept",
        [((height, bins), f32)] * (nt // 2),
        [],
        place,
        stacked,
        ratio,
        scalars=1,
    )
    crossed = [exchanged(block, "tm", 1) for block in away]

    def message_of(index, *extra):
        (message,) = call(
            message_kernel,
            "message",
            [((height + 16, bins), f32)],
            [],
            bound,
            kept[index],
            crossed[index],
            *extra,
        )
        return message.astype(jnp.float16)

    def sent(message, pairs):
        return lax.ppermute(message, "tm", pairs).astype(f32)

    log_sum = sums[1:2]
    if nt == 8:
        first = [(lap, lap ^ (2 << (lap & 1))) for lap in range(nt)]
        second = [(lap, lap ^ (4 >> (lap & 1))) for lap in range(nt)]
        carried = sent(message_of(0), first)
        direct, log_sum = lax.optimization_barrier((message_of(1), log_sum))
        parts = [sent(direct, first)]
        log_sum = log_sum + exchanged(log_sum, "freq", steps[0])
        carried, log_sum = lax.optimization_barrier((carried, log_sum))
        parts.append(sent(message_of(2, carried), second))
    else:
        log_sum = log_sum + exchanged(log_sum, "freq", steps[0])
        parts = [
            sent(message_of(step - 1), [(lap, lap ^ (2 * step)) for lap in range(nt)])
            for step in range(1, nt // 2)
        ]
    (result,) = call(
        total_kernel, "total", [((height, bins), f32)], [], kept[-1], crossed[-1], *parts
    )
    for step in steps[1:]:
        log_sum = log_sum + exchanged(log_sum, "freq", step)
    frame_loss = jnp.log(sums[0]) - log_sum[0] / sums[2]
    return (frame_loss, result)


def solution(mesh):
    placed = (
        P("freq", "tm"),
        P("freq"),
        P("freq"),
        P("tm"),
        P(None, "freq"),
        P(None, "tm"),
        P(None, None, "tm"),
        P(),
        P("freq", None),
    )
    return jax.shard_map(
        on_device, mesh=mesh, in_specs=placed, out_specs=(P("tm"), P("tm", "freq")), check_vma=False
    )
```
